256 devices in a mesh: mem: 2 (over x_lo), lat: 8 (over y, x_hi), lon: 16 (over z, core).
Axes of the slice: x: 4 (x_hi: 2, x_lo: 2; x = x_hi * 2 + x_lo), y: 4, z: 8, core: 2. Of those that a mesh axis runs over, the one named last changes fastest.
Arguments:
- latent_field: bfloat16 [176, 704, 512], P('lat', 'lon', 'mem'), parts along dimension 2, may hold values from -6 to 6
- norm_gain: float32 [2, 256], replicated, may hold values from 0.1 to 1.9
- mixing: bfloat16 [2, 9, 256, 256], replicated, may hold values from -0.375 to 0.375
- kernel_psi: bfloat16 [2, 9, 176, 3, 45], P(None, None, 'lat'), may hold values from -0.625 to 0.625
- lon_reach: int32 [176], P('lat'), may hold values from 0 to 22, as said below
Outputs:
- latent_out: bfloat16 [176, 704, 512], P('lat', 'lon', 'mem'), parts along dimension 2
The draws below stay inside these ranges and needn't reach their ends.
There are 2 independent parts, one for each index of `mem`. The reference program is written for one: setup_inputs(seed, part) draws one part's arguments, and reference() takes and returns one part's arrays. A program takes and returns all parts, laid end to end along the dimension named above; an argument that names none is the same for every part. Nothing has to cross between parts.
Inputs may be any that keep to these rules, and one draw needn't show every extreme that they name: `lon_reach`: the number of longitude cells on either side that the kernel reaches in each row; the first and the last row reach 22.
All inputs are finite; a program needn't handle non-finite values.
Results may differ from the reference program's by a relative error of at most 0.0056.
Values may be sent and summed in bfloat16 or wider, within the bound.
No kernel may reach another device: no remote copies, remote signals or barrier semaphores. Data moves between devices by JAX's collectives and lax.ppermute only.
A program may use at most 192 MiB of HBM per device.

```python
import math
import jax
import jax.numpy as jnp
from jax import lax

C = 256
K = 9
BLOCKS = 2
HMAX = 22
COLS_DEV = 44
NLAT = 176
NLON = 704


def draw_lon_reach(key, part):
    key = jax.random.fold_in(key, 7)
    row_index = jnp.arange(NLAT, dtype=jnp.int32)
    random_part = jax.random.randint(key, (NLAT,), 0, HMAX + 1, dtype=jnp.int32)
    to_pole = jnp.minimum(row_index, NLAT - 1 - row_index)
    reach = jnp.maximum(random_part, HMAX - 4 * to_pole)
    reach = jnp.where(to_pole == 0, HMAX, reach)
    return jnp.clip(reach, 0, HMAX).astype(jnp.int32)


def field_levels(key, offset_scale, channel_spread, common_spread):
    key_offset, key_channel, key_common = jax.random.split(key, 3)
    sector_total = 8
    offset = offset_scale * jax.random.normal(key_offset, (C,), jnp.float32)
    channel_log = jax.random.uniform(key_channel, (sector_total, C), jnp.float32, -channel_spread, channel_spread)
    common_log = jax.random.uniform(key_common, (sector_total, 1), jnp.float32, -common_spread, common_spread)
    level = jnp.exp(channel_log + common_log)
    sector_of = jnp.arange(NLON, dtype=jnp.int32) * sector_total // NLON
    return (offset, jnp.take(level, sector_of, axis=0))


def draw_latent_field(key, part):
    key = jax.random.fold_in(key, 11)
    key_base, key_levels = jax.random.split(key, 2)
    base = jax.random.normal(key_base, (NLAT, NLON, C), jnp.float32)
    offset, column_level = field_levels(key_levels, 0.8, 0.8, 0.35)
    field = offset[None, None, :] + column_level[None, :, :] * base
    return jnp.clip(field, -6.0, 6.0).astype(jnp.bfloat16)


def block_scale(rng, dims, cuts, low, largest):
    level = 1.0
    for position, shards_of in cuts:
        draws = jax.random.uniform(jax.random.fold_in(jax.random.fold_in(rng, 6), position), (shards_of,), jnp.float32, low / len(cuts), largest / len(cuts))
        level = level * jnp.repeat(jnp.exp(draws), dims[position] // shards_of).reshape((-1,) + (1,) * (len(dims) - 1 - position))
    return level


def bell_draw(rng, shape, deviation, most, shards=(), kind=jnp.bfloat16):
    factor_of = block_scale(rng, shape, shards, -0.22, 0.18) if shards else 1.0
    entries = jax.random.normal(rng, shape, jnp.float32) * deviation * factor_of
    return jnp.minimum(jnp.maximum(entries, -most), most).astype(kind)


def setup_inputs(seed: int = 0, part: int = 0) -> dict:
    arg_keys = jax.random.split(jax.random.key(seed), 6)
    own_keys = jax.random.split(jax.random.fold_in(arg_keys[5], part), 6)
    latent_field = draw_latent_field(jax.random.fold_in(jax.random.fold_in(arg_keys[5], part), 71), part)
    norm_gain = jnp.clip(1.0 + 0.18 * jax.random.normal(arg_keys[1], (BLOCKS, C), jnp.float32), 0.1, 1.9)
    mixing = bell_draw(arg_keys[2], (BLOCKS, K, C, C), C ** -0.5, 0.375)
    kernel_psi = bell_draw(arg_keys[3], (BLOCKS, K, NLAT, 3, 2 * HMAX + 1), (1.0 / (3 * K * HMAX) ** 0.5), 0.625, ((2, 8),))
    lon_reach = draw_lon_reach(jax.random.fold_in(arg_keys[5], 71), part)
    return {"latent_field": latent_field, "norm_gain": norm_gain, "mixing": mixing, "kernel_psi": kernel_psi, "lon_reach": lon_reach}


def area_weights():
    row_index = jnp.arange(NLAT).astype(jnp.float32)
    return jnp.cos(math.pi * (row_index + 0.5) / NLAT - math.pi / 2)

def normalize(current, gain_row):
    values = current.astype(jnp.float32)
    weights = area_weights()
    total_weight = NLON * jnp.sum(weights)
    weighted = weights[:, None, None]
    channel_mean = lax.optimization_barrier(jnp.sum(weighted * values, axis=(0, 1))) / total_weight
    channel_second = lax.optimization_barrier(jnp.sum(weighted * values * values, axis=(0, 1))) / total_weight
    inverse = lax.rsqrt(channel_second - channel_mean * channel_mean + 1e-05)
    return ((values - channel_mean) * inverse * gain_row).astype(jnp.bfloat16)

def band_matrix(psi_block, reach_rows, columns):
    width = columns + 2 * HMAX
    offset = jnp.arange(width, dtype=jnp.int32)[None, :] - jnp.arange(columns, dtype=jnp.int32)[:, None]
    tap_index = jnp.arange(2 * HMAX + 1, dtype=jnp.int32)
    onehot = (offset[:, :, None] == tap_index[None, None, :]).astype(jnp.float32)
    inside = (offset >= 0) & (offset <= 2 * HMAX)
    allowed = inside[None] & (jnp.abs(offset - HMAX)[None] <= reach_rows[:, None, None])
    banded = jnp.einsum('kirt,abt->kirab', psi_block.astype(jnp.float32), onehot, precision=lax.Precision.HIGHEST)
    return jnp.where(allowed[None, :, None], banded, 0.0)

def latent_block(current, gain_row, mixing_block, psi_block, lon_reach):
    normed = normalize(current, gain_row)
    joined = jnp.transpose(mixing_block, (1, 0, 2)).reshape(C, K * C)
    mixed = jnp.dot(normed.reshape(-1, C), joined, preferred_element_type=jnp.float32)
    mixed = mixed.astype(jnp.bfloat16).reshape(NLAT, NLON, K * C)
    wrapped = jnp.concatenate([mixed[:, NLON - HMAX:], mixed, mixed[:, :HMAX]], axis=1)
    padded = jnp.pad(wrapped, ((1, 1), (0, 0), (0, 0)))
    band_mats = band_matrix(psi_block, lon_reach, COLS_DEV)
    width = COLS_DEV + 2 * HMAX

    def one_tile(tile_index):
        piece = lax.dynamic_slice_in_dim(padded, tile_index * COLS_DEV, width, 1)
        piece = piece.reshape(NLAT + 2, width, K, C).astype(jnp.float32)
        convolved = jnp.zeros((NLAT, COLS_DEV, C), jnp.float32)
        for shift in range(3):
            convolved = convolved + jnp.einsum('kiab,ibkc->iac', band_mats[:, :, shift], piece[shift:shift + NLAT])
        return convolved
    tiles = lax.map(one_tile, jnp.arange(NLON // COLS_DEV, dtype=jnp.int32))
    convolved = jnp.transpose(tiles, (1, 0, 2, 3)).reshape(NLAT, NLON, C)
    return (current.astype(jnp.float32) + jax.nn.gelu(convolved)).astype(jnp.bfloat16)

def reference(latent_field, norm_gain, mixing, kernel_psi, lon_reach):
    current = latent_field
    for layer in range(BLOCKS):
        current = latent_block(current, norm_gain[layer], mixing[layer], kernel_psi[layer], lon_reach)
    return current
```

```python
import functools
import math

import jax
import jax.numpy as jnp
from jax import lax
from jax.experimental import pallas as pl
from jax.experimental.pallas import tpu as pltpu
from jax.sharding import Mesh, PartitionSpec as P

BLOCKS = 2
HMAX = 22
TAPS = 2 * HMAX + 1
TILE = 16
SPAN = 64
LAT = ("y", "xh")
LON = ("z", "core")
F32 = jnp.float32
BF16 = jnp.bfloat16
VMEM_LIMIT = 56 * 1024 * 1024


def area_weight(row, n_lat):
    return jnp.cos(math.pi * (row.astype(F32) + 0.5) / n_lat - math.pi / 2)


def sums_kernel(x_ref, w_ref, out_ref):
    rows, _, chans = x_ref.shape

    def add_row(i, carry):
        first, second = carry
        v = x_ref[i].astype(F32)
        w = w_ref[i]
        return (
            first + w * jnp.sum(v, axis=0, keepdims=True),
            second + w * jnp.sum(v * v, axis=0, keepdims=True),
        )

    zero = jnp.zeros((1, chans), F32)
    first, second = lax.fori_loop(0, rows, add_row, (zero, zero))
    out_ref[0:1] = first
    out_ref[1:2] = second


def band_kernel(taps_ref, band_ref):
    pairs, _, basis, _ = taps_ref.shape

    def one_pair(p, _):
        for ri in range(2):
            for k in range(basis):
                for half in range(2):
                    lanes = slice(128 * half, 128 * half + 128)
                    line = taps_ref[p, ri, k : k + 1, lanes]
                    spread = jnp.broadcast_to(line, (TILE, 128))
                    moved = pltpu.roll(spread, 0, 1, stride=1, stride_axis=0)
                    at = (ri * basis + k) * TILE
                    band_ref[p, at : at + TILE, lanes] = moved.astype(BF16)
        return 0

    lax.fori_loop(0, pairs, one_pair, 0)


def gain_of(gathered_ref, gain_ref, total_weight):
    total = jnp.sum(gathered_ref[...], axis=0)
    mean = total[0:1] / total_weight
    inverse = lax.rsqrt(total[1:2] / total_weight - mean * mean + 1e-05)
    return mean, inverse, gain_ref[...]


def convolve(u_ref, band_ref, s_ref, rows, cols):
    basis = band_ref.shape[1] // (2 * TILE)
    chans = u_ref.shape[2]
    tiles = cols // TILE

    def one_pair(p, _):
        band = band_ref[p]
        for t in range(tiles):
            window = u_ref[pl.ds(2 * p, 4), TILE * t : TILE * t + SPAN, :]
            window = window.reshape(4 * SPAN, chans)
            s = jnp.dot(band, window, preferred_element_type=F32).astype(BF16)
            for ri in range(2):
                for k in range(basis):
                    at = (ri * basis + k) * TILE
                    s_ref[2 * p + ri, TILE * t : TILE * t + TILE, k * chans : (k + 1) * chans] = s[
                        at : at + TILE
                    ]
        return 0

    lax.fori_loop(0, rows // 2, one_pair, 0)


def first_kernel(
    n_lat, n_lon, place_ref, w_ref, left_right_z, own_ref, left_right_core, gathered_ref, gain_ref,
    band_ref, mix_ref, out_ref, sums_ref, u_ref, res_ref, s_ref,
):
    rows_in, width, chans = own_ref.shape
    rows, cols, _ = out_ref.shape
    total_weight = w_ref[rows]
    mean, inverse, gain = gain_of(gathered_ref, gain_ref, total_weight)
    core = place_ref[1]
    top = place_ref[0]

    def one_row(r, _):
        from_z = left_right_z[r].astype(F32)
        from_core = left_right_core[r].astype(F32)
        own = own_ref[r].astype(F32)
        left = jnp.where(core == 0, from_z, from_core)
        right = jnp.where(core == 0, from_core, from_z)
        pad = jnp.zeros((u_ref.shape[1] - 3 * width, chans), F32)
        full = jnp.concatenate([left, own, right, pad], axis=0)
        here = top + r
        inside = (here >= 0) & (here < n_lat)
        u = jnp.where(inside, (full - mean) * inverse * gain, 0.0)
        u_ref[r] = u.astype(BF16)
        res = jnp.concatenate([left[HMAX:], own, right[:HMAX], pad[: cols - 2 * width]], axis=0)
        res_ref[r] = res.astype(BF16)
        return 0

    lax.fori_loop(0, rows_in, one_row, 0)
    convolve(u_ref, band_ref, s_ref, rows, cols)
    column = lax.broadcasted_iota(jnp.int32, (cols, chans), 0)
    mine = (column >= HMAX) & (column < HMAX + width)
    group = 3

    def mix_rows(g, carry):
        first, second = carry
        lhs = s_ref[pl.ds(group * g, group)].reshape(group * cols, s_ref.shape[2])
        conv = jnp.dot(lhs, mix_ref[...], preferred_element_type=F32)
        grown = jax.nn.gelu(conv).reshape(group, cols, chans)
        for n in range(group):
            i = group * g + n
            new = (res_ref[i + 1].astype(F32) + grown[n]).astype(BF16)
            out_ref[i] = new
            v = jnp.where(mine, new.astype(F32), 0.0)
            w = w_ref[i]
            first = first + w * jnp.sum(v, axis=0, keepdims=True)
            second = second + w * jnp.sum(v * v, axis=0, keepdims=True)
        return first, second

    zero = jnp.zeros((1, chans), F32)
    first, second = lax.fori_loop(0, rows // group, mix_rows, (zero, zero))
    sums_ref[0:1] = first
    sums_ref[1:2] = second


def second_kernel(
    n_lat, n_lon, place_ref, w_ref, x_ref, gathered_ref, gain_ref, band_ref, mix_ref, out_ref,
    u_ref, s_ref,
):
    rows_in, wide, chans = x_ref.shape
    rows, cols, _ = out_ref.shape
    cols_pad = s_ref.shape[1]
    total_weight = w_ref[rows_in]
    mean, inverse, gain = gain_of(gathered_ref, gain_ref, total_weight)
    top = place_ref[0] + 1

    def one_row(r, _):
        here = top + r
        inside = (here >= 0) & (here < n_lat)
        u = jnp.where(inside, (x_ref[r].astype(F32) - mean) * inverse * gain, 0.0)
        u_ref[r] = u.astype(BF16)
        return 0

    lax.fori_loop(0, rows_in, one_row, 0)
    convolve(u_ref, band_ref, s_ref, rows, cols_pad)
    group = 11

    def mix_rows(g, _):
        lhs = s_ref[pl.ds(group * g, group)].reshape(group * cols_pad, s_ref.shape[2])
        conv = jnp.dot(lhs, mix_ref[...], preferred_element_type=F32)
        grown = jax.nn.gelu(conv).reshape(group, cols_pad, chans)
        for n in range(group):
            i = group * g + n
            res = x_ref[i + 1].astype(F32)[HMAX : HMAX + cols]
            out_ref[i] = (res + grown[n, :cols]).astype(BF16)
        return 0

    lax.fori_loop(0, rows // group, mix_rows, 0)


def vmem():
    return pl.BlockSpec(memory_space=pltpu.VMEM)


def smem():
    return pl.BlockSpec(memory_space=pltpu.SMEM)


def call(kernel, out_shape, ins, scratch=(), flops=0, moved=0):
    return pl.pallas_call(
        kernel,
        out_shape=out_shape,
        in_specs=[smem() if s else vmem() for s in ins],
        out_specs=jax.tree.map(lambda _: vmem(), out_shape),
        scratch_shapes=list(scratch),
        compiler_params=pltpu.CompilerParams(vmem_limit_bytes=VMEM_LIMIT),
        cost_estimate=pl.CostEstimate(flops=flops, bytes_accessed=moved, transcendentals=0),
    )


def swap_pairs(count, first):
    pairs = []
    for i in range(first, count - 1, 2):
        pairs += [(i, i + 1), (i + 1, i)]
    return pairs


def spread_taps(masked):
    basis, rows, _, _ = masked.shape
    lines = jnp.pad(masked.astype(F32), ((0, 0), (0, 0), (0, 0), (0, SPAN - TAPS)))
    lines = lines.reshape(basis, rows // 2, 2, 3 * SPAN)
    even = jnp.pad(lines[:, :, 0], ((0, 0), (0, 0), (0, SPAN)))
    odd = jnp.pad(lines[:, :, 1], ((0, 0), (0, 0), (SPAN, 0)))
    return jnp.transpose(jnp.stack([even, odd], axis=2), (1, 2, 0, 3))


def bands_of(masked):
    taps = spread_taps(masked)
    pairs, _, basis, _ = taps.shape
    shape = jax.ShapeDtypeStruct((pairs, 2 * basis * TILE, 4 * SPAN), BF16)
    return call(band_kernel, shape, [False], flops=10**6, moved=4 * 10**6)(taps)


def gather_sums(sums):
    sums = sums + lax.ppermute(sums, "core", [(0, 1), (1, 0)])
    axes = ("y", "xh", "z")
    count = math.prod(lax.axis_size(a) for a in axes)
    return lax.all_to_all(jnp.broadcast_to(sums[None], (count,) + sums.shape), axes, 0, 0)


def local(x, norm_gain, mixing, kernel_psi, lon_reach):
    rows, cols, chans = x.shape
    basis = mixing.shape[1]
    n_lat = rows * lax.axis_size("y") * lax.axis_size("xh")
    n_lon = cols * lax.axis_size("z") * lax.axis_size("core")
    lat = lax.axis_index("y") * 2 + lax.axis_index("xh")
    xh = lax.axis_index("xh")
    core = lax.axis_index("core")
    top = lat * rows
    all_weights = area_weight(jnp.arange(n_lat, dtype=jnp.int32), n_lat)
    total_weight = n_lon * jnp.sum(all_weights)
    own_rows = top + jnp.arange(rows, dtype=jnp.int32)
    weights = area_weight(own_rows, n_lat)
    zero = jnp.zeros((1,), F32)
    wide_weights = jnp.concatenate([zero, weights, zero, total_weight[None]])
    place = jnp.stack([top - 2, core]).astype(jnp.int32)

    tap = jnp.arange(TAPS, dtype=jnp.int32) - HMAX
    keep = jnp.abs(tap)[None] <= lon_reach[:, None]
    masked = jnp.where(keep[None, None, :, None, :], kernel_psi, jnp.zeros((), BF16))

    def lat_message(edge_rows, tap_row):
        flat = tap_row.reshape(-1)
        count = -(-flat.shape[0] // chans)
        flat = jnp.pad(flat, (0, count * chans - flat.shape[0])).reshape(count, chans)
        return jnp.concatenate([edge_rows.reshape(-1, chans), flat], axis=0)

    low = lat_message(x[:2], masked[0, :, 0])
    high = lat_message(x[rows - 2 :], masked[0, :, rows - 1])
    got_a = lax.ppermute(jnp.where(xh == 0, high, low), LAT, swap_pairs(8, 0))
    got_b = lax.ppermute(jnp.where(xh == 0, low, high), LAT, swap_pairs(8, 1))
    above = jnp.where(xh == 0, got_b, got_a)
    below = jnp.where(xh == 0, got_a, got_b)

    def taps_from(message):
        return message[2 * cols :].reshape(-1)[: basis * 3 * TAPS].reshape(basis, 1, 3, TAPS)

    tall = jnp.concatenate(
        [above[: 2 * cols].reshape(2, cols, chans), x, below[: 2 * cols].reshape(2, cols, chans)],
        axis=0,
    )
    from_core = lax.ppermute(tall, "core", [(0, 1), (1, 0)])
    ring = []
    for z in range(8):
        a, b = 2 * z + 1, (2 * z + 2) % 16
        ring += [(a, b), (b, a)]
    from_z = lax.ppermute(tall, LON, ring)

    sums_shape = jax.ShapeDtypeStruct((2, chans), F32)
    sums = call(sums_kernel, sums_shape, [False, True], moved=10**6, flops=10**6)(x, weights)
    gathered = gather_sums(sums)

    bands_second = bands_of(masked[1])
    bands_first = bands_of(jnp.concatenate([taps_from(above), masked[0], taps_from(below)], axis=1))

    wide = 96
    tall_rows = rows + 4
    deep = basis * chans
    x1, sums1 = call(
        functools.partial(first_kernel, n_lat, n_lon),
        (jax.ShapeDtypeStruct((rows + 2, wide, chans), BF16), sums_shape),
        [True, True] + [False] * 7,
        [
            pltpu.VMEM((tall_rows, 144, chans), BF16),
            pltpu.VMEM((tall_rows, wide, chans), BF16),
            pltpu.VMEM((rows + 2, wide, deep), BF16),
        ],
        flops=5 * 10**9,
        moved=10**7,
    )(
        place, wide_weights, from_z, tall, from_core, gathered, norm_gain[0:1], bands_first,
        mixing[0].reshape(deep, chans),
    )
    gathered1 = gather_sums(sums1)
    return call(
        functools.partial(second_kernel, n_lat, n_lon),
        jax.ShapeDtypeStruct((rows, cols, chans), BF16),
        [True, True] + [False] * 5,
        [pltpu.VMEM((rows + 2, wide, chans), BF16), pltpu.VMEM((rows, 48, deep), BF16)],
        flops=25 * 10**8,
        moved=5 * 10**6,
    )(
        place, wide_weights, x1, gathered1, norm_gain[1:2], bands_second,
        mixing[1].reshape(deep, chans),
    )


def solution(mesh):
    split = Mesh(mesh.devices.reshape(2, 4, 2, 8, 2), ("mem", "y", "xh", "z", "core"))
    placed = (P(LAT, LON, "mem"), P(), P(), P(None, None, LAT, None, None), P(LAT))
    return jax.shard_map(
        local, mesh=split, in_specs=placed, out_specs=P(LAT, LON, "mem"), check_vma=False
    )
```

```python
import functools
import math

import jax
import jax.numpy as jnp
import numpy as np
from jax import lax
from jax.experimental import pallas as pl
from jax.experimental.pallas import tpu as pltpu
from jax.sharding import Mesh, PartitionSpec as P

BLOCKS = 2
HMAX = 22
TAPS = 2 * HMAX + 1
TILE = 16
SPAN = 64
ROWS = 22
COLS = 44
CHANS = 256
BASIS = 9
N_LAT = 176
N_LON = 704
WIDE = 96
DEEP = BASIS * CHANS
HIGH = BASIS * TILE
LAT = ("y", "xh")
LON = ("z", "core")
F32 = jnp.float32
BF16 = jnp.bfloat16
VMEM_LIMIT = 24 * 1024 * 1024
WEIGHTS = np.cos(np.pi * (np.arange(N_LAT) + 0.5) / N_LAT - np.pi / 2)
TOTAL = float(N_LON * WEIGHTS.sum())


def lat_index():
    return lax.axis_index("y") * 2 + lax.axis_index("xh")


def area_weights(weight_ref):
    row = lax.broadcasted_iota(jnp.int32, (24, CHANS), 0)
    angle = ((lat_index() * ROWS + row).astype(F32) + 0.5) * (math.pi / N_LAT)
    weight = jnp.where(row < ROWS, jnp.sin(angle), 0.0)
    weight_ref[...] = weight
    return COLS * jnp.sum(weight, axis=0, keepdims=True)


def start_all(pairs, sems):
    copies = [pltpu.make_async_copy(s, t, sems.at[n]) for n, (s, t) in enumerate(pairs)]
    for copy in copies:
        copy.start()
    return copies


def put_band(rows, odd, store):
    halves = [None, None]
    for r in range(3):
        place = r + odd
        moved = pltpu.roll(rows[r], SPAN * (place % 2), 1, stride=1, stride_axis=0)
        half = place // 2
        halves[half] = moved if halves[half] is None else halves[half] + moved
    store(slice(0, 128), halves[0].astype(BF16))
    store(slice(128, 256), halves[1].astype(BF16))


def spread(line):
    return jnp.broadcast_to(line, (TILE, 128))


def taps_of(reach_ref, psi_ref, block, i, k):
    tap = lax.broadcasted_iota(jnp.int32, (1, 128), 1) - HMAX
    near = jnp.abs(tap) <= reach_ref[i]
    row = lat_index() * ROWS + i - 1
    taps = []
    for r in range(3):
        keep = near & (row + r >= 0) & (row + r < N_LAT)
        line = jnp.where(keep, psi_ref[k, i, r].astype(F32)[block : block + 1], 0.0)
        taps.append(jnp.broadcast_to(line, (TILE, 128)))
    return taps


def make_bands(reach_ref, psi_ref, block, band_ref, tap_sum_ref, line_ref, sends=()):
    def two_rows(p, _):
        for n in range(2):
            i = 2 * p + n
            for k in range(BASIS):

                def store(lanes, value):
                    band_ref[i, k * TILE : (k + 1) * TILE, lanes] = value

                rows = taps_of(reach_ref, psi_ref, block, i, k)
                put_band(rows, (n + 1 - block) % 2, store)
                line_ref[k, pl.ds(i, 1)] = (rows[0] + rows[1] + rows[2])[0:1]
        return 0

    if sends:
        lax.fori_loop(0, 6, two_rows, 0)
        sends[0].start()
        lax.fori_loop(6, ROWS // 2, two_rows, 0)
        sends[1].start()
    else:
        lax.fori_loop(0, ROWS // 2, two_rows, 0)
    for k in range(BASIS):
        whole = jnp.sum(line_ref[k], axis=1, keepdims=True)
        tap_sum_ref[:, k * CHANS : (k + 1) * CHANS] = jnp.broadcast_to(whole, (ROWS, CHANS))


def prep_kernel(
    reach_ref, x_any, psi_any, sums_ref, mean_ref, edge_ref, band_any, tap_sum_any,
    x_ref, psi_ref, band_ref, tap_sum_ref, line_ref, weight_ref, sems,
):
    x_in, psi_in = start_all([(x_any, x_ref), (psi_any, psi_ref)], sems)
    whole = area_weights(weight_ref)
    x_in.wait()

    def add_row(i, carry):
        first, second = carry
        v = x_ref[i].astype(F32)
        wv = weight_ref[pl.ds(i, 1)] * v
        return first + wv, second + wv * v

    zero = jnp.zeros((COLS, CHANS), F32)
    first, second = lax.fori_loop(0, ROWS, add_row, (zero, zero))
    first = jnp.sum(first, axis=0, keepdims=True)
    sums_ref[0:1] = first
    sums_ref[1:2] = jnp.sum(second, axis=0, keepdims=True)
    mean_ref[...] = first / whole
    psi_in.wait()
    for n in range(2):
        for k in range(BASIS):
            taps = taps_of(reach_ref, psi_ref, 0, n * (ROWS - 1), k)
            for r in range(3):
                edge_ref[n, 3 * k + r : 3 * k + r + 1] = taps[r][0:1]
    half = ROWS // 2
    parts = [(band_ref.at[pl.ds(n * half, half)], band_any.at[pl.ds(n * half, half)]) for n in range(2)]
    sends = [pltpu.make_async_copy(*part, sems.at[2 + n]) for n, part in enumerate(parts)]
    make_bands(reach_ref, psi_ref, 0, band_ref, tap_sum_ref, line_ref, sends)
    sends.append(pltpu.make_async_copy(tap_sum_ref, tap_sum_any, sems.at[4]))
    sends[-1].start()
    for send in sends:
        send.wait()


def message_kernel(
    z_ref, own_any, core_ref, edge_ref, sums_ref, other_ref, a_ref, b_ref, both_ref, sems
):
    xh = lax.axis_index("xh")
    pairs = []
    for n, out in enumerate((a_ref, b_ref)):
        start = jnp.where(xh == n, ROWS - 2, 0)
        pairs.append((own_any.at[pl.ds(start, 2)], out.at[pl.ds(2, 2)]))
    copies = start_all(pairs, sems)
    for n, out in enumerate((a_ref, b_ref)):
        taps = jnp.where(xh == n, edge_ref[1], edge_ref[0])
        start = jnp.where(xh == n, ROWS - 2, 0)
        out[0:2] = z_ref[pl.ds(start, 2)]
        out[4:6] = core_ref[pl.ds(start, 2)]
        out[6] = jnp.zeros((COLS, CHANS), BF16)
        out[6, 0:32, 0:128] = jnp.concatenate([taps, jnp.zeros((5, 128), F32)], axis=0).astype(BF16)
    both_ref[...] = jnp.broadcast_to((sums_ref[...] + other_ref[...])[None], both_ref.shape)
    for copy in copies:
        copy.wait()


def add_kernel(sums_ref, other_ref, both_ref):
    both_ref[...] = jnp.broadcast_to((sums_ref[...] + other_ref[...])[None], both_ref.shape)


def convolve(p, band, u_ref, s_ref, tiles):
    for t in range(tiles):
        window = u_ref[pl.ds(2 * p, 4), TILE * t : TILE * t + SPAN, :].reshape(4 * SPAN, CHANS)
        s = jnp.dot(band, window, preferred_element_type=F32).astype(BF16)
        for ri in range(2):
            for k in range(BASIS):
                at = (ri * BASIS + k) * TILE
                s_ref[2 * p + ri, TILE * t : TILE * t + TILE, k * CHANS : (k + 1) * CHANS] = s[
                    at : at + TILE
                ]


def first_conv_kernel(
    mean_ref, z_ref, core_ref, a_ref, b_ref, own_any, band_any, s_any, tap_sum_any, res_any,
    tap_sum_ref, res_ref, u_ref, edge_ref, own_ref, band_ref, s_ref, in_sems, out_sems,
):
    own_in, band_in = start_all([(own_any, own_ref), (band_any, band_ref)], in_sems)
    xh, core = lax.axis_index("xh"), lax.axis_index("core")
    local_mean = mean_ref[...]

    def put_row(r, from_z, own, from_core):
        from_z, own, from_core = from_z.astype(F32), own.astype(F32), from_core.astype(F32)
        left = jnp.where(core == 0, from_z, from_core)
        right = jnp.where(core == 0, from_core, from_z)
        pad = jnp.zeros((12, CHANS), F32)
        u_ref[r] = (jnp.concatenate([left, own, right, pad], axis=0) - local_mean).astype(BF16)
        res = jnp.concatenate([left[HMAX:], own, right[:HMAX], pad[:8]], axis=0)
        return res.astype(BF16)

    def own_row(i, _):
        res_ref[i + 1] = put_row(i + 2, z_ref[i], own_ref[i], core_ref[i])
        return 0

    own_in.wait()
    lax.fori_loop(0, ROWS, own_row, 0)
    band_in.wait()

    def rim(piece, upper):
        use_b = (xh == 0) if upper else (xh == 1)
        return jnp.where(use_b, b_ref[piece].astype(F32), a_ref[piece].astype(F32))

    for upper in (True, False):
        for j in range(2):
            res = put_row(
                j if upper else ROWS + 2 + j, rim(j, upper), rim(2 + j, upper), rim(4 + j, upper)
            )
            if j == (1 if upper else 0):
                res_ref[0 if upper else ROWS + 1] = res
        place = 0 if upper else 1
        lines = rim(6, upper)[:, :128]
        for k in range(BASIS):

            def store(lanes, value):
                edge_ref[place, k * TILE : (k + 1) * TILE, lanes] = value

            rows = [spread(lines[3 * k + r : 3 * k + r + 1]) for r in range(3)]
            put_band(rows, place, store)
            whole = jnp.sum((rows[0] + rows[1] + rows[2])[0:1], axis=1, keepdims=True)
            tap_sum_ref[place : place + 1, k * CHANS : (k + 1) * CHANS] = jnp.broadcast_to(
                whole, (1, CHANS)
            )

    tiles = WIDE // TILE
    rest = [
        pltpu.make_async_copy(tap_sum_ref, tap_sum_any, in_sems.at[2]),
        pltpu.make_async_copy(res_ref, res_any, in_sems.at[3]),
    ]
    for send_rest in rest:
        send_rest.start()

    def send(p):
        at = pl.ds(2 * p, 2)
        return pltpu.make_async_copy(s_ref.at[at], s_any.at[at], out_sems.at[p])

    def one_pair(p, _):
        band = band_ref[pl.ds(2 * p - 1, 2)].reshape(2 * HIGH, 4 * SPAN)
        convolve(p, band, u_ref, s_ref, tiles)
        send(p).start()
        return 0

    convolve(0, jnp.concatenate([edge_ref[0], band_ref[0]], axis=0), u_ref, s_ref, tiles)
    send(0).start()
    lax.fori_loop(1, ROWS // 2, one_pair, 0)
    convolve(ROWS // 2, jnp.concatenate([band_ref[ROWS - 1], edge_ref[1]], axis=0), u_ref, s_ref, tiles)
    send(ROWS // 2).start()

    def end(p, _):
        send(p).wait()
        return 0

    lax.fori_loop(0, ROWS // 2 + 1, end, 0)
    for send_rest in rest:
        send_rest.wait()


def scale_of(gathered_ref, gain):
    total = jnp.sum(gathered_ref[...], axis=0)
    mean = total[0:1] / TOTAL
    scale = lax.rsqrt(total[1:2] / TOTAL - mean * mean + 1e-05) * gain
    diagonal = lax.broadcasted_iota(jnp.int32, (CHANS, CHANS), 0) == lax.broadcasted_iota(
        jnp.int32, (CHANS, CHANS), 1
    )
    return mean, jnp.sum(jnp.where(diagonal, scale, 0.0), axis=1, keepdims=True)


def scale_mixing(column, mix_ref, scaled_ref):
    for k in range(BASIS):
        scaled_ref[k * CHANS : (k + 1) * CHANS] = (mix_ref[k].astype(F32) * column).astype(BF16)


def shift_rows(tap_sum, shift, scaled_ref):
    lhs = tap_sum * jnp.concatenate([shift] * BASIS, axis=1)
    high = lhs.astype(BF16)
    low = (lhs - high.astype(F32)).astype(BF16)
    scaled = scaled_ref[...]
    return jnp.dot(high, scaled, preferred_element_type=F32) + jnp.dot(
        low, scaled, preferred_element_type=F32
    )


def first_mix_kernel(
    gathered_ref, local_mean_ref, gain_any, edge_sum_any, mix_any, s_any, tap_sum_any, res_any,
    mid_any, scaled_any, shift_any, sums_ref, new_mean_ref,
    gain_ref, edge_sum_ref, shift_ref, mix_ref, s_ref, tap_sum_ref, res_ref, mid_ref, scaled_ref, weight_ref, in_sems, out_sems,
):
    mid = 4 * TILE
    parts = (6, 8, 8)
    spans = [(sum(parts[:g]), parts[g]) for g in range(len(parts))]
    of_mid = pl.ds(TILE, mid)
    pairs = [
        (mix_any.at[0], mix_ref),
        (tap_sum_any, tap_sum_ref),
        (res_any.at[pl.ds(1, ROWS), of_mid], res_ref),
        (gain_any, gain_ref),
        (edge_sum_any, edge_sum_ref),
    ] + [(s_any.at[pl.ds(at + 1, n), of_mid], s_ref.at[pl.ds(at, n)]) for at, n in spans]
    mix_in, tap_in, res_in, gain_in, edge_in, *s_in = [
        pltpu.make_async_copy(s, t, in_sems.at[n]) for n, (s, t) in enumerate(pairs)
    ]
    for now in (gain_in, mix_in, tap_in, edge_in, s_in[0]):
        now.start()
    whole = area_weights(weight_ref)
    gain_in.wait()
    mean, column = scale_of(gathered_ref, gain_ref[0:1])
    shift = local_mean_ref[...] - mean
    mix_in.wait()
    for later in (s_in[1], res_in, s_in[2]):
        later.start()
    scale_mixing(column, mix_ref, scaled_ref)
    send_scaled = pltpu.make_async_copy(scaled_ref, scaled_any, out_sems.at[0])
    send_scaled.start()
    tap_in.wait()
    edge_in.wait()
    shift_ref[0:ROWS] = shift_rows(tap_sum_ref[...], shift, scaled_ref)
    shift_ref[ROWS : ROWS + 2] = shift_rows(edge_sum_ref[...], shift, scaled_ref)
    column = lax.broadcasted_iota(jnp.int32, (mid, CHANS), 0) + TILE
    mine = (column >= HMAX) & (column < HMAX + COLS)
    first = second = jnp.zeros((mid, CHANS), F32)
    send_shift = pltpu.make_async_copy(shift_ref, shift_any, out_sems.at[4])
    send_shift.start()
    sends = [send_scaled, send_shift]
    for g, (at, n) in enumerate(spans):
        s_in[g].wait()
        lhs = s_ref[at : at + n].reshape(n * mid, DEEP)
        conv = jnp.dot(lhs, scaled_ref[...], preferred_element_type=F32).reshape(n, mid, CHANS)
        if g == 0:
            res_in.wait()
        for i in range(at, at + n):
            grown = jax.nn.gelu(conv[i - at] + shift_ref[i : i + 1])
            new = (res_ref[i].astype(F32) + grown).astype(BF16)
            mid_ref[i] = new
            v = jnp.where(mine, new.astype(F32), 0.0)
            wv = weight_ref[i : i + 1] * v
            first, second = first + wv, second + wv * v
        span = pl.ds(at, n)
        sends.append(pltpu.make_async_copy(mid_ref.at[span], mid_any.at[span], out_sems.at[1 + g]))
        sends[-1].start()
    first = jnp.sum(first, axis=0, keepdims=True)
    sums_ref[0:1] = first
    sums_ref[1:2] = jnp.sum(second, axis=0, keepdims=True)
    new_mean_ref[...] = first / whole
    for send in sends:
        send.wait()


def second_conv_kernel(
    reach_ref, mean_ref, shift_any, psi_any, scaled_any, res_any, mid_any, s_any, tap_sum_any, out_any,
    tap_sum_ref, shift_ref, u_ref, s_ref, rows_ref, out_ref, psi_ref, scaled_ref, res_ref, mid_ref, band_ref, line_ref,
    in_sems, out_sems,
):
    psi_in, *fetches, mid_in = start_all(
        [(psi_any, psi_ref), (scaled_any, scaled_ref), (res_any, res_ref)]
        + [
            (s_any.at[pl.ds(1, ROWS), pl.ds(n * (WIDE - TILE), TILE)], s_ref.at[n])
            for n in range(2)
        ]
        + [(s_any.at[n * (ROWS + 1)], rows_ref.at[n]) for n in range(2)]
        + [(shift_any, shift_ref), (mid_any, mid_ref)],
        in_sems,
    )
    local_mean = mean_ref[...]
    psi_in.wait()
    make_bands(reach_ref, psi_ref, 1, band_ref, tap_sum_ref, line_ref)
    tap_out = pltpu.make_async_copy(tap_sum_ref, tap_sum_any, in_sems.at[10])
    tap_out.start()

    for fetch in fetches:
        fetch.wait()
    for left in range(2):
        at = slice(left * (WIDE - TILE), left * (WIDE - TILE) + TILE)
        lhs = s_ref[left].reshape(ROWS * TILE, DEEP)
        conv = jnp.dot(lhs, scaled_ref[...], preferred_element_type=F32).reshape(ROWS, TILE, CHANS)
        for i in range(ROWS):
            grown = jax.nn.gelu(conv[i] + shift_ref[i : i + 1])
            new = (res_ref[i + 1, at].astype(F32) + grown).astype(BF16).astype(F32)
            u_ref[i + 1, at] = (new - local_mean).astype(BF16)
    lhs = rows_ref[...].reshape(2 * WIDE, DEEP)
    conv = jnp.dot(lhs, scaled_ref[...], preferred_element_type=F32).reshape(2, WIDE, CHANS)
    for n in range(2):
        e = n * (ROWS + 1)
        grown = jax.nn.gelu(conv[n] + shift_ref[ROWS + n : ROWS + n + 1])
        new = (res_ref[e].astype(F32) + grown).astype(BF16).astype(F32)
        u_ref[e] = (new - local_mean).astype(BF16)

    mid_in.wait()

    def mid_row(i, _):
        u_ref[i + 1, TILE : 5 * TILE] = (mid_ref[i].astype(F32) - local_mean).astype(BF16)
        return 0

    lax.fori_loop(0, ROWS, mid_row, 0)

    def one_pair(p, _):
        band = band_ref[pl.ds(2 * p, 2)].reshape(2 * HIGH, 4 * SPAN)
        convolve(p, band, u_ref, out_ref, 3)
        send(p).start()
        return 0

    def send(p):
        at = pl.ds(2 * p, 2)
        return pltpu.make_async_copy(out_ref.at[at], out_any.at[at], out_sems.at[p])

    def end(p, _):
        send(p).wait()
        return 0

    lax.fori_loop(0, ROWS // 2, one_pair, 0)
    lax.fori_loop(0, ROWS // 2, end, 0)
    tap_out.wait()


def second_mix_kernel(
    gathered_ref, local_mean_ref, gain_any, mix_any, s_any, tap_sum_any, mid_any, out_any,
    gain_ref, mix_ref, s_ref, tap_sum_ref, mid_ref, scaled_ref, shift_ref, out_ref, in_sems, out_sems,
):
    cols = 3 * TILE
    parts = (6, 8, 8)
    spans = [(sum(parts[:g]), parts[g]) for g in range(len(parts))]
    pairs = [
        (mix_any.at[1], mix_ref),
        (tap_sum_any, tap_sum_ref),
        (mid_any, mid_ref),
        (gain_any, gain_ref),
    ] + [
        (s_any.at[pl.ds(at, n)], s_ref.at[pl.ds(at, n)]) for at, n in spans
    ]
    mix_in, tap_in, mid_in, gain_in, *s_in = [
        pltpu.make_async_copy(s, t, in_sems.at[n]) for n, (s, t) in enumerate(pairs)
    ]
    for now in (gain_in, mix_in, tap_in, s_in[0]):
        now.start()
    gain_in.wait()
    mean, column = scale_of(gathered_ref, gain_ref[1:2])
    shift = local_mean_ref[...] - mean
    mix_in.wait()
    for later in (s_in[1], mid_in, s_in[2]):
        later.start()
    scale_mixing(column, mix_ref, scaled_ref)
    tap_in.wait()
    shift_ref[...] = shift_rows(tap_sum_ref[...], shift, scaled_ref)
    sends = []
    for g, (at, n) in enumerate(spans):
        s_in[g].wait()
        lhs = s_ref[at : at + n].reshape(n * cols, DEEP)
        conv = jnp.dot(lhs, scaled_ref[...], preferred_element_type=F32).reshape(n, cols, CHANS)
        if g == 0:
            mid_in.wait()
        for i in range(at, at + n):
            grown = jax.nn.gelu(conv[i - at] + shift_ref[i : i + 1])
            res = mid_ref[i].astype(F32)[HMAX - TILE : HMAX - TILE + COLS]
            out_ref[i] = (res + grown[:COLS]).astype(BF16)
        span = pl.ds(at, n)
        sends.append(pltpu.make_async_copy(out_ref.at[span], out_any.at[span], out_sems.at[g]))
        sends[-1].start()
    for send in sends:
        send.wait()


def shape(*dims, dtype=BF16):
    return jax.ShapeDtypeStruct(dims, dtype)


SMEM = pl.BlockSpec(memory_space=pltpu.SMEM)
VMEM = pl.BlockSpec(memory_space=pltpu.VMEM)
HBM = pl.BlockSpec(memory_space=pltpu.HBM)


def call(kernel, ins, outs, scratch=(), flops=10**6):
    run = pl.pallas_call(
        kernel,
        out_shape=[pltpu.HBM(o.shape, o.dtype) if spec is HBM else o for o, spec in outs],
        in_specs=ins,
        out_specs=[spec for _, spec in outs],
        scratch_shapes=list(scratch),
        compiler_params=pltpu.CompilerParams(vmem_limit_bytes=VMEM_LIMIT),
        cost_estimate=pl.CostEstimate(flops=flops, bytes_accessed=10**6, transcendentals=0),
    )

    def placed(*values):
        return run(
            *[
                pltpu.with_memory_space_constraint(v, pltpu.HBM) if spec is HBM else v
                for v, spec in zip(values, ins)
            ]
        )

    return placed


def swap_pairs(count, first):
    pairs = []
    for i in range(first, count - 1, 2):
        pairs += [(i, i + 1), (i + 1, i)]
    return pairs


def from_other_core(v):
    return lax.ppermute(v, "core", [(0, 1), (1, 0)])


def gather(both):
    return lax.all_to_all(both, ("y", "xh", "z"), 0, 0)


def buffer(*dims):
    return pltpu.VMEM(dims, BF16)


def semaphores(count):
    return pltpu.SemaphoreType.DMA((count,))


def floats(*dims):
    return pltpu.VMEM(dims, F32)


def local(x, norm_gain, mixing, kernel_psi, lon_reach):
    peers = lax.axis_size("y") * lax.axis_size("xh") * lax.axis_size("z")
    sums_out = (shape(2, CHANS, dtype=F32), VMEM)
    mean_out = (shape(1, CHANS, dtype=F32), VMEM)
    both_out = (shape(peers, 2, CHANS, dtype=F32), VMEM)
    tap_sum_out = (shape(ROWS, DEEP, dtype=F32), HBM)
    mid_cols, own_cols = 4 * TILE, 3 * TILE

    from_core = from_other_core(x)
    ring = []
    for z in range(8):
        a, b = 2 * z + 1, (2 * z + 2) % 16
        ring += [(a, b), (b, a)]
    from_z = lax.ppermute(x, LON, ring)

    psi = jnp.transpose(kernel_psi, (1, 2, 3, 0, 4))
    psi = jnp.pad(psi, ((0, 0),) * 4 + ((0, 128 - TAPS),))
    sums, mean, edge, band1, tap_sum1 = call(
        prep_kernel,
        [SMEM, HBM, HBM],
        [
            sums_out,
            mean_out,
            (shape(2, 3 * BASIS, 128, dtype=F32), VMEM),
            (shape(ROWS, HIGH, 4 * SPAN), HBM),
            tap_sum_out,
        ],
        [
            buffer(ROWS, COLS, CHANS),
            buffer(BASIS, ROWS, 3, BLOCKS, 128),
            buffer(ROWS, HIGH, 4 * SPAN),
            floats(ROWS, DEEP),
            floats(BASIS, ROWS, 128),
            floats(24, CHANS),
            semaphores(5),
        ],
    )(lon_reach, x, psi)

    message = (shape(7, COLS, CHANS), VMEM)
    to_a, to_b, both = call(
        message_kernel, [VMEM, HBM] + [VMEM] * 4, [message, message, both_out], [semaphores(2)]
    )(from_z, x, from_core, edge, sums, from_other_core(sums))
    got_a = lax.ppermute(to_a, LAT, swap_pairs(8, 0))
    got_b = lax.ppermute(to_b, LAT, swap_pairs(8, 1))
    gathered = gather(both)

    s1, edge_sum, res = call(
        first_conv_kernel,
        [VMEM] * 5 + [HBM] * 2,
        [
            (shape(ROWS + 2, WIDE, DEEP), HBM),
            (shape(2, DEEP, dtype=F32), HBM),
            (shape(ROWS + 2, WIDE, CHANS), HBM),
        ],
        [
            floats(2, DEEP),
            buffer(ROWS + 2, WIDE, CHANS),
            buffer(ROWS + 4, 144, CHANS),
            buffer(2, HIGH, 4 * SPAN),
            buffer(ROWS, COLS, CHANS),
            buffer(ROWS, HIGH, 4 * SPAN),
            buffer(ROWS + 2, WIDE, DEEP),
            semaphores(4),
            semaphores(12),
        ],
        flops=4 * 10**9,
    )(mean, from_z, from_core, got_a, got_b, x, band1)
    mid, scaled, shift, sums1, mean1 = call(
        first_mix_kernel,
        [VMEM] * 2 + [HBM] * 6,
        [
            (shape(ROWS, mid_cols, CHANS), HBM),
            (shape(DEEP, CHANS), HBM),
            (shape(ROWS + 2, CHANS, dtype=F32), HBM),
            sums_out,
            mean_out,
        ],
        [
            floats(BLOCKS, CHANS),
            floats(2, DEEP),
            floats(ROWS + 2, CHANS),
            buffer(BASIS, CHANS, CHANS),
            buffer(ROWS, mid_cols, DEEP),
            floats(ROWS, DEEP),
            buffer(ROWS, mid_cols, CHANS),
            buffer(ROWS, mid_cols, CHANS),
            buffer(DEEP, CHANS),
            floats(24, CHANS),
            semaphores(8),
            semaphores(5),
        ],
        flops=2 * 10**9,
    )(gathered, mean, norm_gain, edge_sum, mixing, s1, tap_sum1, res)
    (both1,) = call(add_kernel, [VMEM, VMEM], [both_out])(sums1, from_other_core(sums1))
    gathered1 = gather(both1)
    tap_sum2, s2 = call(
        second_conv_kernel,
        [SMEM, VMEM] + [HBM] * 6,
        [tap_sum_out, (shape(ROWS, own_cols, DEEP), HBM)],
        [
            floats(ROWS, DEEP),
            floats(ROWS + 2, CHANS),
            buffer(ROWS + 2, WIDE, CHANS),
            buffer(2, ROWS, TILE, DEEP),
            buffer(2, WIDE, DEEP),
            buffer(ROWS, own_cols, DEEP),
            buffer(BASIS, ROWS, 3, BLOCKS, 128),
            buffer(DEEP, CHANS),
            buffer(ROWS + 2, WIDE, CHANS),
            buffer(ROWS, mid_cols, CHANS),
            buffer(ROWS, HIGH, 4 * SPAN),
            floats(BASIS, ROWS, 128),
            semaphores(11),
            semaphores(11),
        ],
        flops=3 * 10**9,
    )(lon_reach, mean1, shift, psi, scaled, res, mid, s1)
    (out,) = call(
        second_mix_kernel,
        [VMEM] * 2 + [HBM] * 5,
        [(shape(ROWS, COLS, CHANS), HBM)],
        [
            floats(BLOCKS, CHANS),
            buffer(BASIS, CHANS, CHANS),
            buffer(ROWS, own_cols, DEEP),
            floats(ROWS, DEEP),
            buffer(ROWS, mid_cols, CHANS),
            buffer(DEEP, CHANS),
            floats(ROWS, CHANS),
            buffer(ROWS, COLS, CHANS),
            semaphores(7),
            semaphores(3),
        ],
        flops=2 * 10**9,
    )(gathered1, mean1, norm_gain, mixing, s2, tap_sum2, mid)
    return out


def solution(mesh):
    split = Mesh(mesh.devices.reshape(2, 4, 2, 8, 2), ("mem", "y", "xh", "z", "core"))
    placed = (P(LAT, LON, "mem"), P(), P(), P(None, None, LAT, None, None), P(LAT))
    return jax.shard_map(
        local, mesh=split, in_specs=placed, out_specs=P(LAT, LON, "mem"), check_vma=False
    )
```

```python
import functools
import math

import jax
import jax.numpy as jnp
import numpy as np
from jax import lax
from jax.experimental import pallas as pl
from jax.experimental.pallas import tpu as pltpu
from jax.sharding import Mesh, PartitionSpec as P

BLOCKS = 2
HMAX = 22
TAPS = 2 * HMAX + 1
TILE = 16
SPAN = 64
ROWS = 22
COLS = 44
CHANS = 256
BASIS = 9
N_LAT = 176
N_LON = 704
WIDE = 96
DEEP = BASIS * CHANS
HIGH = BASIS * TILE
LAT = ("y", "xh")
LON = ("z", "core")
F32 = jnp.float32
BF16 = jnp.bfloat16
VMEM_LIMIT = 28 * 1024 * 1024
WEIGHTS = np.cos(np.pi * (np.arange(N_LAT) + 0.5) / N_LAT - np.pi / 2)
TOTAL = float(N_LON * WEIGHTS.sum())


def lat_index():
    return lax.axis_index("y") * 2 + lax.axis_index("xh")


def area_weights(weight_ref):
    row = lax.broadcasted_iota(jnp.int32, (24, CHANS), 0)
    angle = ((lat_index() * ROWS + row).astype(F32) + 0.5) * (math.pi / N_LAT)
    weight = jnp.where(row < ROWS, jnp.sin(angle), 0.0)
    weight_ref[...] = weight
    return COLS * jnp.sum(weight, axis=0, keepdims=True)


def start_all(pairs, sems):
    copies = [pltpu.make_async_copy(s, t, sems.at[n]) for n, (s, t) in enumerate(pairs)]
    for copy in copies:
        copy.start()
    return copies


def put_band(rows, odd, store):
    halves = [None, None]
    for r in range(3):
        place = r + odd
        moved = pltpu.roll(rows[r], SPAN * (place % 2), 1, stride=1, stride_axis=0)
        half = place // 2
        halves[half] = moved if halves[half] is None else halves[half] + moved
    store(slice(0, 128), halves[0].astype(BF16))
    store(slice(128, 256), halves[1].astype(BF16))


def spread(line):
    return jnp.broadcast_to(line, (TILE, 128))


def taps_of(reach_ref, psi_ref, block, i, k, at=None):
    tap = lax.broadcasted_iota(jnp.int32, (1, TAPS), 1) - HMAX
    rest = jnp.zeros((1, 128 - TAPS), F32)
    near = jnp.abs(tap) <= reach_ref[i]
    row = lat_index() * ROWS + i - 1
    taps = []
    for r in range(3):
        keep = near & (row + r >= 0) & (row + r < N_LAT)
        line = jnp.where(keep, psi_ref[k, i if at is None else at, r].astype(F32)[block : block + 1], 0.0)
        taps.append(jnp.broadcast_to(jnp.concatenate([line, rest], axis=1), (TILE, 128)))
    return taps


def make_bands(reach_ref, psi_ref, block, band_ref, tap_sum_ref, line_ref, sends):
    def two_rows(p, _):
        for n in range(2):
            i = 2 * p + n
            for k in range(BASIS):

                def store(lanes, value):
                    band_ref[i, k * TILE : (k + 1) * TILE, lanes] = value

                rows = taps_of(reach_ref, psi_ref, block, i, k)
                put_band(rows, (n + 1 - block) % 2, store)
                line_ref[k, pl.ds(i, 1)] = (rows[0] + rows[1] + rows[2])[0:1]
        return 0

    lax.fori_loop(0, 6, two_rows, 0)
    sends[0].start()
    lax.fori_loop(6, ROWS // 2, two_rows, 0)
    sends[1].start()
    for k in range(BASIS):
        whole = jnp.sum(line_ref[k], axis=1, keepdims=True)
        tap_sum_ref[:, k * CHANS : (k + 1) * CHANS] = jnp.broadcast_to(whole, (ROWS, CHANS))


def sums_kernel(
    x_any, reach_any, psi_any, sums_ref, mean_ref, edge_ref, x_ref, reach_ref, psi_ref, weight_ref, sems
):
    ends = (0, ROWS - 1)
    reach_in, *psi_in = [
        pltpu.make_async_copy(s, t, sems.at[2 + n])
        for n, (s, t) in enumerate(
            [(reach_any, reach_ref)] + [(psi_any.at[:, i], psi_ref.at[:, n]) for n, i in enumerate(ends)]
        )
    ]
    for fetch in (reach_in, *psi_in):
        fetch.start()
    half = ROWS // 2
    parts = start_all([(x_any.at[pl.ds(n * half, half)], x_ref.at[pl.ds(n * half, half)]) for n in range(2)], sems)
    whole = area_weights(weight_ref)

    def add_row(i, carry):
        first, second = carry
        v = x_ref[i].astype(F32)
        wv = weight_ref[pl.ds(i, 1)] * v
        return first + wv, second + wv * v

    zero = jnp.zeros((COLS, CHANS), F32)
    parts[0].wait()
    carry = lax.fori_loop(0, half, add_row, (zero, zero))
    parts[1].wait()
    first, second = lax.fori_loop(half, ROWS, add_row, carry)
    first = jnp.sum(first, axis=0, keepdims=True)
    sums_ref[0:1] = first
    sums_ref[1:2] = jnp.sum(second, axis=0, keepdims=True)
    mean_ref[...] = first / whole
    for fetch in (reach_in, *psi_in):
        fetch.wait()
    for n, i in enumerate(ends):
        for k in range(BASIS):
            taps = taps_of(reach_ref, psi_ref, 0, i, k, n)
            for r in range(3):
                edge_ref[n, 3 * k + r : 3 * k + r + 1] = taps[r][0:1]


def prep_kernel(
    message_ref, reach_any, psi_any, band1_any, tap_sum1_any, band2_any, tap_sum2_any,
    reach_ref, psi_ref, band1_ref, tap_sum1_ref, band2_ref, tap_sum2_ref, line_ref, sems,
):
    psi_in, reach_in = start_all([(psi_any, psi_ref), (reach_any, reach_ref)], sems)
    psi_in.wait()
    reach_in.wait()
    outs = ((band1_ref, band1_any, tap_sum1_ref, tap_sum1_any), (band2_ref, band2_any, tap_sum2_ref, tap_sum2_any))
    half = ROWS // 2
    sends = []
    for block, (band_ref, band_any, tap_sum_ref, tap_sum_any) in enumerate(outs):
        pairs = [(band_ref.at[pl.ds(n * half, half)], band_any.at[pl.ds(n * half, half)]) for n in range(2)]
        pairs.append((tap_sum_ref, tap_sum_any))
        mine = [pltpu.make_async_copy(*pair, sems.at[3 + 3 * block + n]) for n, pair in enumerate(pairs)]
        make_bands(reach_ref, psi_ref, block, band_ref, tap_sum_ref, line_ref, mine)
        mine[2].start()
        sends += mine
    for send in sends:
        send.wait()


def message_kernel(z_ref, own_any, core_ref, edge_ref, both_ref, a_ref, b_ref, sems):
    xh = lax.axis_index("xh")
    starts = [jnp.where(xh == n, ROWS - 2, 0) for n in range(2)]
    copies = start_all(
        [(own_any.at[pl.ds(s, 2)], out.at[pl.ds(2, 2)]) for s, out in zip(starts, (a_ref, b_ref))], sems
    )
    for n, out in enumerate((a_ref, b_ref)):
        taps = jnp.where(xh == n, edge_ref[1], edge_ref[0])
        out[0:2] = z_ref[pl.ds(starts[n], 2)]
        out[4:6] = core_ref[pl.ds(starts[n], 2)]
        out[6] = jnp.zeros((COLS, CHANS), BF16)
        out[6, 0:32, 0:128] = jnp.concatenate([taps, jnp.zeros((5, 128), F32)], axis=0).astype(BF16)
    for copy in copies:
        copy.wait()


def add_kernel(sums_ref, other_ref, both_ref):
    both_ref[...] = jnp.broadcast_to((sums_ref[...] + other_ref[...])[None], both_ref.shape)


def convolve(p, band, u_ref, s_ref, tiles):
    for t in range(tiles):
        window = u_ref[pl.ds(2 * p, 4), TILE * t : TILE * t + SPAN, :].reshape(4 * SPAN, CHANS)
        s = jnp.dot(band, window, preferred_element_type=F32).astype(BF16)
        for ri in range(2):
            for k in range(BASIS):
                at = (ri * BASIS + k) * TILE
                s_ref[2 * p + ri, TILE * t : TILE * t + TILE, k * CHANS : (k + 1) * CHANS] = s[
                    at : at + TILE
                ]


def scale_of(gathered_ref, gain):
    total = jnp.sum(gathered_ref[...], axis=0)
    mean = total[0:1] / TOTAL
    scale = lax.rsqrt(total[1:2] / TOTAL - mean * mean + 1e-05) * gain
    diagonal = lax.broadcasted_iota(jnp.int32, (CHANS, CHANS), 0) == lax.broadcasted_iota(
        jnp.int32, (CHANS, CHANS), 1
    )
    return mean, jnp.sum(jnp.where(diagonal, scale, 0.0), axis=1, keepdims=True)


def scale_mixing(column, mix_ref, scaled_ref):
    for k in range(BASIS):
        scaled_ref[k * CHANS : (k + 1) * CHANS] = (mix_ref[k].astype(F32) * column).astype(BF16)


def shift_rows(tap_sum, shift, scaled_ref):
    lhs = tap_sum * jnp.concatenate([shift] * BASIS, axis=1)
    high = lhs.astype(BF16)
    low = (lhs - high.astype(F32)).astype(BF16)
    scaled = scaled_ref[...]
    return jnp.dot(high, scaled, preferred_element_type=F32) + jnp.dot(
        low, scaled, preferred_element_type=F32
    )


def first_kernel(
    local_mean_ref, a_ref, b_ref, gathered_ref, z_any, core_any, own_any, band_any, mix_any, gain_any, tap_sum_any,
    s_any, res_any, mid_ref, shift_ref, scaled_any, sums_ref, new_mean_ref,
    res_ref, mix_ref, gain_ref, tap_sum_ref, edge_sum_ref, u_ref, edge_ref, z_ref, core_ref, own_ref, band_ref,
    s_ref, scaled_ref, weight_ref, in_sems, out_sems,
):
    z_in, core_in, own_in, band_in, mix_in, gain_in, tap_in = start_all(
        [
            (z_any, z_ref),
            (core_any, core_ref),
            (own_any, own_ref),
            (band_any, band_ref),
            (mix_any.at[0], mix_ref),
            (gain_any, gain_ref),
            (tap_sum_any, tap_sum_ref),
        ],
        in_sems,
    )
    xh, core = lax.axis_index("xh"), lax.axis_index("core")
    local_mean = local_mean_ref[...]

    def put_row(r, from_z, own, from_core):
        from_z, own, from_core = from_z.astype(F32), own.astype(F32), from_core.astype(F32)
        left = jnp.where(core == 0, from_z, from_core)
        right = jnp.where(core == 0, from_core, from_z)
        pad = jnp.zeros((12, CHANS), F32)
        u_ref[r] = (jnp.concatenate([left, own, right, pad], axis=0) - local_mean).astype(BF16)
        res = jnp.concatenate([left[HMAX:], own, right[:HMAX], pad[:8]], axis=0)
        return res.astype(BF16)

    def own_row(i, _):
        res_ref[i + 1] = put_row(i + 2, z_ref[i], own_ref[i], core_ref[i])
        return 0

    z_in.wait()
    core_in.wait()
    own_in.wait()
    lax.fori_loop(0, ROWS, own_row, 0)
    band_in.wait()

    def rim(piece, upper):
        use_b = (xh == 0) if upper else (xh == 1)
        return jnp.where(use_b, b_ref[piece].astype(F32), a_ref[piece].astype(F32))

    for upper in (True, False):
        for j in range(2):
            res = put_row(
                j if upper else ROWS + 2 + j, rim(j, upper), rim(2 + j, upper), rim(4 + j, upper)
            )
            if j == (1 if upper else 0):
                res_ref[0 if upper else ROWS + 1] = res
        place = 0 if upper else 1
        lines = rim(6, upper)[:, :128]
        for k in range(BASIS):

            def store(lanes, value):
                edge_ref[place, k * TILE : (k + 1) * TILE, lanes] = value

            rows = [spread(lines[3 * k + r : 3 * k + r + 1]) for r in range(3)]
            put_band(rows, place, store)
            whole = jnp.sum((rows[0] + rows[1] + rows[2])[0:1], axis=1, keepdims=True)
            edge_sum_ref[place : place + 1, k * CHANS : (k + 1) * CHANS] = jnp.broadcast_to(
                whole, (1, CHANS)
            )

    tiles = WIDE // TILE
    def one_pair(p, _):
        band = band_ref[pl.ds(2 * p - 1, 2)].reshape(2 * HIGH, 4 * SPAN)
        convolve(p, band, u_ref, s_ref, tiles)
        return 0

    convolve(0, jnp.concatenate([edge_ref[0], band_ref[0]], axis=0), u_ref, s_ref, tiles)
    lax.fori_loop(1, ROWS // 2, one_pair, 0)
    convolve(ROWS // 2, jnp.concatenate([band_ref[ROWS - 1], edge_ref[1]], axis=0), u_ref, s_ref, tiles)

    strips = [(pl.ds(1, ROWS), pl.ds(n * (WIDE - TILE), TILE)) for n in range(2)]
    strips += [(pl.ds(n * (ROWS + 1), 1),) for n in range(2)]
    rim = start_all([(s_ref.at[at], s_any.at[at]) for at in strips] + [(res_ref, res_any)], out_sems)
    mid = 4 * TILE
    parts = (11, 11)
    spans = [(sum(parts[:g]), parts[g]) for g in range(len(parts))]
    whole = area_weights(weight_ref)
    gain_in.wait()
    mix_in.wait()
    mean, column = scale_of(gathered_ref, gain_ref[0:1])
    shift = local_mean - mean
    scale_mixing(column, mix_ref, scaled_ref)
    send_scaled = pltpu.make_async_copy(scaled_ref, scaled_any, out_sems.at[5])
    send_scaled.start()
    tap_in.wait()
    shift_ref[0:ROWS] = shift_rows(tap_sum_ref[...], shift, scaled_ref)
    shift_ref[ROWS : ROWS + 2] = shift_rows(edge_sum_ref[...], shift, scaled_ref)
    column = lax.broadcasted_iota(jnp.int32, (mid, CHANS), 0) + TILE
    mine = (column >= HMAX) & (column < HMAX + COLS)
    first = second = jnp.zeros((mid, CHANS), F32)
    for at, n in spans:
        lhs = s_ref[at + 1 : at + 1 + n, TILE : TILE + mid].reshape(n * mid, DEEP)
        conv = jnp.dot(lhs, scaled_ref[...], preferred_element_type=F32).reshape(n, mid, CHANS)
        for i in range(at, at + n):
            grown = jax.nn.gelu(conv[i - at] + shift_ref[i : i + 1])
            new = (res_ref[i + 1, TILE : TILE + mid].astype(F32) + grown).astype(BF16)
            mid_ref[i] = new
            v = jnp.where(mine, new.astype(F32), 0.0)
            wv = weight_ref[i : i + 1] * v
            first, second = first + wv, second + wv * v
    first = jnp.sum(first, axis=0, keepdims=True)
    sums_ref[0:1] = first
    sums_ref[1:2] = jnp.sum(second, axis=0, keepdims=True)
    new_mean_ref[...] = first / whole
    send_scaled.wait()
    for send in rim:
        send.wait()


def second_conv_kernel(
    mean_ref, shift_ref, mid_ref, res_any, band_any, scaled_any, s_any, mix_any,
    out_any, mix_ref, res_ref, u_ref, s_ref, rows_ref, out_ref, scaled_ref, band_ref, in_sems, out_sems,
):
    *fetches, band_in, mix_in = start_all(
        [(scaled_any, scaled_ref), (res_any, res_ref)]
        + [
            (s_any.at[pl.ds(1, ROWS), pl.ds(n * (WIDE - TILE), TILE)], s_ref.at[n])
            for n in range(2)
        ]
        + [(s_any.at[n * (ROWS + 1)], rows_ref.at[n]) for n in range(2)]
        + [(band_any, band_ref), (mix_any.at[1], mix_ref)],
        in_sems,
    )
    local_mean = mean_ref[...]

    def mid_row(i, _):
        u_ref[i + 1, TILE : 5 * TILE] = (mid_ref[i].astype(F32) - local_mean).astype(BF16)
        return 0

    lax.fori_loop(0, ROWS, mid_row, 0)

    for fetch in fetches:
        fetch.wait()
    for left in range(2):
        at = slice(left * (WIDE - TILE), left * (WIDE - TILE) + TILE)
        lhs = s_ref[left].reshape(ROWS * TILE, DEEP)
        conv = jnp.dot(lhs, scaled_ref[...], preferred_element_type=F32).reshape(ROWS, TILE, CHANS)
        for i in range(ROWS):
            grown = jax.nn.gelu(conv[i] + shift_ref[i : i + 1])
            new = (res_ref[i + 1, at].astype(F32) + grown).astype(BF16).astype(F32)
            u_ref[i + 1, at] = (new - local_mean).astype(BF16)
    lhs = rows_ref[...].reshape(2 * WIDE, DEEP)
    conv = jnp.dot(lhs, scaled_ref[...], preferred_element_type=F32).reshape(2, WIDE, CHANS)
    for n in range(2):
        e = n * (ROWS + 1)
        grown = jax.nn.gelu(conv[n] + shift_ref[ROWS + n : ROWS + n + 1])
        new = (res_ref[e].astype(F32) + grown).astype(BF16).astype(F32)
        u_ref[e] = (new - local_mean).astype(BF16)

    band_in.wait()

    def one_pair(p, _):
        band = band_ref[pl.ds(2 * p, 2)].reshape(2 * HIGH, 4 * SPAN)
        convolve(p, band, u_ref, out_ref, 3)
        send(p).start()
        return 0

    def send(p):
        at = pl.ds(2 * p, 2)
        return pltpu.make_async_copy(out_ref.at[at], out_any.at[at], out_sems.at[p])

    def end(p, _):
        send(p).wait()
        return 0

    lax.fori_loop(0, ROWS // 2, one_pair, 0)
    lax.fori_loop(0, ROWS // 2, end, 0)
    mix_in.wait()


def second_mix_kernel(
    gathered_ref, local_mean_ref, mix_ref, mid_ref, gain_any, s_any, tap_sum_any, out_any,
    gain_ref, s_ref, tap_sum_ref, scaled_ref, shift_ref, out_ref, in_sems, out_sems,
):
    cols = 3 * TILE
    parts = (4, 8, 10)
    spans = [(sum(parts[:g]), parts[g]) for g in range(len(parts))]
    gain_in, tap_in, *s_in = start_all(
        [(gain_any, gain_ref), (tap_sum_any, tap_sum_ref)]
        + [(s_any.at[pl.ds(at, n)], s_ref.at[pl.ds(at, n)]) for at, n in spans],
        in_sems,
    )
    gain_in.wait()
    mean, column = scale_of(gathered_ref, gain_ref[1:2])
    shift = local_mean_ref[...] - mean
    scale_mixing(column, mix_ref, scaled_ref)
    tap_in.wait()
    shift_ref[...] = shift_rows(tap_sum_ref[...], shift, scaled_ref)
    sends = []
    for g, (at, n) in enumerate(spans):
        s_in[g].wait()
        lhs = s_ref[at : at + n].reshape(n * cols, DEEP)
        conv = jnp.dot(lhs, scaled_ref[...], preferred_element_type=F32).reshape(n, cols, CHANS)
        for i in range(at, at + n):
            grown = jax.nn.gelu(conv[i - at] + shift_ref[i : i + 1])
            res = mid_ref[i].astype(F32)[HMAX - TILE : HMAX - TILE + COLS]
            out_ref[i] = (res + grown[:COLS]).astype(BF16)
        span = pl.ds(at, n)
        sends.append(pltpu.make_async_copy(out_ref.at[span], out_any.at[span], out_sems.at[g]))
        sends[-1].start()
    for send in sends:
        send.wait()


def shape(*dims, dtype=BF16):
    return jax.ShapeDtypeStruct(dims, dtype)


SMEM = pl.BlockSpec(memory_space=pltpu.SMEM)
VMEM = pl.BlockSpec(memory_space=pltpu.VMEM)
HBM = pl.BlockSpec(memory_space=pltpu.HBM)
KEPT = pl.BlockSpec(memory_space=pltpu.VMEM)


def call(kernel, ins, outs, scratch=(), flops=10**6):
    def out_shape(o, spec):
        space = {id(HBM): pltpu.HBM, id(KEPT): pltpu.VMEM}.get(id(spec))
        return o if space is None else space(o.shape, o.dtype)

    run = pl.pallas_call(
        kernel,
        out_shape=[out_shape(*o) for o in outs],
        in_specs=ins,
        out_specs=[spec for _, spec in outs],
        scratch_shapes=list(scratch),
        compiler_params=pltpu.CompilerParams(vmem_limit_bytes=VMEM_LIMIT),
        cost_estimate=pl.CostEstimate(flops=flops, bytes_accessed=10**6, transcendentals=0),
    )

    def in_place(v, spec):
        space = {id(HBM): pltpu.HBM, id(KEPT): pltpu.VMEM}.get(id(spec))
        return v if space is None else pltpu.with_memory_space_constraint(v, space)

    return lambda *values: run(*[in_place(v, spec) for v, spec in zip(values, ins)])


def swap_pairs(count, first):
    pairs = []
    for i in range(first, count - 1, 2):
        pairs += [(i, i + 1), (i + 1, i)]
    return pairs


def from_other_core(v):
    return lax.ppermute(v, "core", [(0, 1), (1, 0)])


def gather(both):
    return lax.all_to_all(both, ("y", "xh", "z"), 0, 0)


def buffer(*dims):
    return pltpu.VMEM(dims, BF16)


def semaphores(count):
    return pltpu.SemaphoreType.DMA((count,))


def floats(*dims):
    return pltpu.VMEM(dims, F32)


def local(x, norm_gain, mixing, kernel_psi, lon_reach):
    peers = lax.axis_size("y") * lax.axis_size("xh") * lax.axis_size("z")
    sums_out = (shape(2, CHANS, dtype=F32), VMEM)
    mean_out = (shape(1, CHANS, dtype=F32), VMEM)
    both_out = (shape(peers, 2, CHANS, dtype=F32), VMEM)
    tap_sum_out = (shape(ROWS, DEEP, dtype=F32), HBM)
    mid_cols, own_cols = 4 * TILE, 3 * TILE

    from_core = from_other_core(x)
    ring = []
    for z in range(8):
        a, b = 2 * z + 1, (2 * z + 2) % 16
        ring += [(a, b), (b, a)]
    from_z = lax.ppermute(x, LON, ring)

    psi = jnp.transpose(kernel_psi, (1, 2, 3, 0, 4))
    band_outs = [(shape(ROWS, HIGH, 4 * SPAN), HBM), tap_sum_out]
    edge_out = (shape(2, 3 * BASIS, 128, dtype=F32), VMEM)
    sums, mean, edge = call(
        sums_kernel,
        [HBM, HBM, HBM],
        [sums_out, mean_out, edge_out],
        [
            buffer(ROWS, COLS, CHANS),
            pltpu.SMEM((ROWS,), jnp.int32),
            buffer(BASIS, 2, 3, BLOCKS, TAPS),
            floats(24, CHANS),
            semaphores(5),
        ],
    )(x, lon_reach, psi)
    (both,) = call(add_kernel, [VMEM, VMEM], [both_out])(sums, from_other_core(sums))
    gathered = gather(both)

    message = (shape(7, COLS, CHANS), VMEM)
    to_a, to_b = call(message_kernel, [VMEM, HBM] + [VMEM] * 3, [message, message], [semaphores(2)])(
        from_z, x, from_core, edge, both
    )
    band1, tap_sum1, band2, tap_sum2 = call(
        prep_kernel,
        [VMEM, HBM, HBM],
        band_outs + band_outs,
        [pltpu.SMEM((ROWS,), jnp.int32), buffer(BASIS, ROWS, 3, BLOCKS, TAPS)]
        + [buffer(ROWS, HIGH, 4 * SPAN), floats(ROWS, DEEP)] * 2
        + [floats(BASIS, ROWS, 128), semaphores(9)],
        flops=5 * 10**9,
    )(to_a, lon_reach, psi)
    got_a = lax.ppermute(to_a, LAT, swap_pairs(8, 0))
    got_b = lax.ppermute(to_b, LAT, swap_pairs(8, 1))

    s1, res, mid, shift, scaled, sums1, mean1 = call(
        first_kernel,
        [VMEM] * 4 + [HBM] * 7,
        [
            (shape(ROWS + 2, WIDE, DEEP), HBM),
            (shape(ROWS + 2, WIDE, CHANS), HBM),
            (shape(ROWS, mid_cols, CHANS), KEPT),
            (shape(ROWS + 2, CHANS, dtype=F32), KEPT),
            (shape(DEEP, CHANS), HBM),
            sums_out,
            mean_out,
        ],
        [
            buffer(ROWS + 2, WIDE, CHANS),
            buffer(BASIS, CHANS, CHANS),
            floats(BLOCKS, CHANS),
            floats(ROWS, DEEP),
            floats(2, DEEP),
            buffer(ROWS + 4, 144, CHANS),
            buffer(2, HIGH, 4 * SPAN),
            buffer(ROWS, COLS, CHANS),
            buffer(ROWS, COLS, CHANS),
            buffer(ROWS, COLS, CHANS),
            buffer(ROWS, HIGH, 4 * SPAN),
            buffer(ROWS + 2, WIDE, DEEP),
            buffer(DEEP, CHANS),
            floats(24, CHANS),
            semaphores(7),
            semaphores(6),
        ],
    )(mean, got_a, got_b, gathered, from_z, from_core, x, band1, mixing, norm_gain, tap_sum1)
    (both1,) = call(add_kernel, [VMEM, VMEM], [both_out])(sums1, from_other_core(sums1))
    gathered1 = gather(both1)
    s2, mix2 = call(
        second_conv_kernel,
        [VMEM] + [KEPT] * 2 + [HBM] * 5,
        [(shape(ROWS, own_cols, DEEP), HBM), (shape(BASIS, CHANS, CHANS), KEPT)],
        [
            buffer(ROWS + 2, WIDE, CHANS),
            buffer(ROWS + 2, WIDE, CHANS),
            buffer(2, ROWS, TILE, DEEP),
            buffer(2, WIDE, DEEP),
            buffer(ROWS, own_cols, DEEP),
            buffer(DEEP, CHANS),
            buffer(ROWS, HIGH, 4 * SPAN),
            semaphores(8),
            semaphores(11),
        ],
        flops=9 * 10**9,
    )(mean1, shift, mid, res, band2, scaled, s1, mixing)
    (out,) = call(
        second_mix_kernel,
        [VMEM] * 2 + [KEPT] * 2 + [HBM] * 3,
        [(shape(ROWS, COLS, CHANS), HBM)],
        [
            floats(BLOCKS, CHANS),
            buffer(ROWS, own_cols, DEEP),
            floats(ROWS, DEEP),
            buffer(DEEP, CHANS),
            floats(ROWS, CHANS),
            buffer(ROWS, COLS, CHANS),
            semaphores(5),
            semaphores(3),
        ],
        flops=2 * 10**9,
    )(gathered1, mean1, mix2, mid, norm_gain, s2, tap_sum2)
    return out


def solution(mesh):
    split = Mesh(mesh.devices.reshape(2, 4, 2, 8, 2), ("mem", "y", "xh", "z", "core"))
    placed = (P(LAT, LON, "mem"), P(), P(), P(None, None, LAT, None, None), P(LAT))
    return jax.shard_map(
        local, mesh=split, in_specs=placed, out_specs=P(LAT, LON, "mem"), check_vma=False
    )
```

```python
import functools
import math

import jax
import jax.numpy as jnp
import numpy as np
from jax import lax
from jax.experimental import pallas as pl
from jax.experimental.pallas import tpu as pltpu
from jax.sharding import Mesh, PartitionSpec as P

BLOCKS = 2
HMAX = 22
TAPS = 2 * HMAX + 1
TILE = 16
SPAN = 64
ROWS = 22
COLS = 44
CHANS = 256
BASIS = 9
N_LAT = 176
N_LON = 704
WIDE = 96
DEEP = BASIS * CHANS
HIGH = BASIS * TILE
LAT = ("y", "xh")
LON = ("z", "core")
F32 = jnp.float32
BF16 = jnp.bfloat16
VMEM_LIMIT = 28 * 1024 * 1024
WEIGHTS = np.cos(np.pi * (np.arange(N_LAT) + 0.5) / N_LAT - np.pi / 2)
TOTAL = float(N_LON * WEIGHTS.sum())


def lat_index():
    return lax.axis_index("y") * 2 + lax.axis_index("xh")


def area_weights(weight_ref):
    row = lax.broadcasted_iota(jnp.int32, (24, CHANS), 0)
    angle = ((lat_index() * ROWS + row).astype(F32) + 0.5) * (math.pi / N_LAT)
    weight = jnp.where(row < ROWS, jnp.sin(angle), 0.0)
    weight_ref[...] = weight
    return COLS * jnp.sum(weight, axis=0, keepdims=True)


def start_all(pairs, sems):
    copies = [pltpu.make_async_copy(s, t, sems.at[n]) for n, (s, t) in enumerate(pairs)]
    for copy in copies:
        copy.start()
    return copies


def put_band(rows, odd, store):
    halves = [None, None]
    for r in range(3):
        place = r + odd
        moved = pltpu.roll(rows[r], SPAN * (place % 2), 1, stride=1, stride_axis=0)
        half = place // 2
        halves[half] = moved if halves[half] is None else halves[half] + moved
    store(slice(0, 128), halves[0].astype(BF16))
    store(slice(128, 256), halves[1].astype(BF16))


def spread(line):
    return jnp.broadcast_to(line, (TILE, 128))


def taps_of(reach_ref, psi_ref, block, i, k, at=None):
    tap = lax.broadcasted_iota(jnp.int32, (1, TAPS), 1) - HMAX
    rest = jnp.zeros((1, 128 - TAPS), F32)
    near = jnp.abs(tap) <= reach_ref[i]
    row = lat_index() * ROWS + i - 1
    taps = []
    for r in range(3):
        keep = near & (row + r >= 0) & (row + r < N_LAT)
        line = jnp.where(keep, psi_ref[k, i if at is None else at, r].astype(F32)[block : block + 1], 0.0)
        taps.append(jnp.broadcast_to(jnp.concatenate([line, rest], axis=1), (TILE, 128)))
    return taps


def make_bands(reach_ref, psi_ref, block, band_ref, tap_sum_ref, line_ref, sends):
    def two_rows(p, _):
        for n in range(2):
            i = 2 * p + n
            for k in range(BASIS):

                def store(lanes, value):
                    band_ref[i, k * TILE : (k + 1) * TILE, lanes] = value

                rows = taps_of(reach_ref, psi_ref, block, i, k)
                put_band(rows, (n + 1 - block) % 2, store)
                line_ref[k, pl.ds(i, 1)] = (rows[0] + rows[1] + rows[2])[0:1]
        return 0

    lax.fori_loop(0, 6, two_rows, 0)
    sends[0].start()
    lax.fori_loop(6, ROWS // 2, two_rows, 0)
    sends[1].start()
    for k in range(BASIS):
        whole = jnp.sum(line_ref[k], axis=1, keepdims=True)
        tap_sum_ref[:, k * CHANS : (k + 1) * CHANS] = jnp.broadcast_to(whole, (ROWS, CHANS))


def sums_kernel(
    x_any, reach_any, psi_any, sums_ref, mean_ref, edge_ref, x_ref, reach_ref, psi_ref, weight_ref, sems
):
    ends = (0, ROWS - 1)
    reach_in, *psi_in = [
        pltpu.make_async_copy(s, t, sems.at[2 + n])
        for n, (s, t) in enumerate(
            [(reach_any, reach_ref)] + [(psi_any.at[:, i], psi_ref.at[:, n]) for n, i in enumerate(ends)]
        )
    ]
    for fetch in (reach_in, *psi_in):
        fetch.start()
    half = ROWS // 2
    parts = start_all([(x_any.at[pl.ds(n * half, half)], x_ref.at[pl.ds(n * half, half)]) for n in range(2)], sems)
    whole = area_weights(weight_ref)

    def add_row(i, carry):
        first, second = carry
        v = x_ref[i].astype(F32)
        wv = weight_ref[pl.ds(i, 1)] * v
        return first + wv, second + wv * v

    zero = jnp.zeros((COLS, CHANS), F32)
    parts[0].wait()
    carry = lax.fori_loop(0, half, add_row, (zero, zero))
    parts[1].wait()
    first, second = lax.fori_loop(half, ROWS, add_row, carry)
    first = jnp.sum(first, axis=0, keepdims=True)
    sums_ref[0:1] = first
    sums_ref[1:2] = jnp.sum(second, axis=0, keepdims=True)
    mean_ref[...] = first / whole
    for fetch in (reach_in, *psi_in):
        fetch.wait()
    for n, i in enumerate(ends):
        for k in range(BASIS):
            taps = taps_of(reach_ref, psi_ref, 0, i, k, n)
            for r in range(3):
                edge_ref[n, 3 * k + r : 3 * k + r + 1] = taps[r][0:1]


def prep_kernel(
    message_ref, reach_any, psi_any, band1_any, tap_sum1_any, band2_any, tap_sum2_any,
    reach_ref, psi_ref, band1_ref, tap_sum1_ref, band2_ref, tap_sum2_ref, line_ref, sems,
):
    psi_in, reach_in = start_all([(psi_any, psi_ref), (reach_any, reach_ref)], sems)
    psi_in.wait()
    reach_in.wait()
    outs = ((band1_ref, band1_any, tap_sum1_ref, tap_sum1_any), (band2_ref, band2_any, tap_sum2_ref, tap_sum2_any))
    half = ROWS // 2
    sends = []
    for block, (band_ref, band_any, tap_sum_ref, tap_sum_any) in enumerate(outs):
        pairs = [(band_ref.at[pl.ds(n * half, half)], band_any.at[pl.ds(n * half, half)]) for n in range(2)]
        pairs.append((tap_sum_ref, tap_sum_any))
        mine = [pltpu.make_async_copy(*pair, sems.at[3 + 3 * block + n]) for n, pair in enumerate(pairs)]
        make_bands(reach_ref, psi_ref, block, band_ref, tap_sum_ref, line_ref, mine)
        mine[2].start()
        sends += mine
    for send in sends:
        send.wait()


def message_kernel(z_ref, own_any, core_ref, edge_ref, both_ref, a_ref, b_ref, sems):
    xh = lax.axis_index("xh")
    starts = [jnp.where(xh == n, ROWS - 2, 0) for n in range(2)]
    copies = start_all(
        [(own_any.at[pl.ds(s, 2)], out.at[pl.ds(2, 2)]) for s, out in zip(starts, (a_ref, b_ref))], sems
    )
    for n, out in enumerate((a_ref, b_ref)):
        taps = jnp.where(xh == n, edge_ref[1], edge_ref[0])
        out[0:2] = z_ref[pl.ds(starts[n], 2)]
        out[4:6] = core_ref[pl.ds(starts[n], 2)]
        out[6] = jnp.zeros((COLS, CHANS), BF16)
        out[6, 0:32, 0:128] = jnp.concatenate([taps, jnp.zeros((5, 128), F32)], axis=0).astype(BF16)
    for copy in copies:
        copy.wait()


def add_kernel(sums_ref, other_ref, both_ref):
    both_ref[...] = jnp.broadcast_to((sums_ref[...] + other_ref[...])[None], both_ref.shape)


def convolve(p, band, u_ref, s_ref, tiles):
    for t in range(tiles):
        window = u_ref[pl.ds(2 * p, 4), TILE * t : TILE * t + SPAN, :].reshape(4 * SPAN, CHANS)
        s = jnp.dot(band, window, preferred_element_type=F32).astype(BF16)
        for ri in range(2):
            for k in range(BASIS):
                at = (ri * BASIS + k) * TILE
                s_ref[2 * p + ri, TILE * t : TILE * t + TILE, k * CHANS : (k + 1) * CHANS] = s[
                    at : at + TILE
                ]


def scale_of(gathered_ref, gain):
    total = jnp.sum(gathered_ref[...], axis=0)
    mean = total[0:1] / TOTAL
    scale = lax.rsqrt(total[1:2] / TOTAL - mean * mean + 1e-05) * gain
    diagonal = lax.broadcasted_iota(jnp.int32, (CHANS, CHANS), 0) == lax.broadcasted_iota(
        jnp.int32, (CHANS, CHANS), 1
    )
    return mean, jnp.sum(jnp.where(diagonal, scale, 0.0), axis=1, keepdims=True)


def scale_mixing(column, mix_ref, scaled_ref):
    for k in range(BASIS):
        scaled_ref[k * CHANS : (k + 1) * CHANS] = (mix_ref[k].astype(F32) * column).astype(BF16)


def shift_rows(tap_sum, shift, scaled_ref):
    lhs = tap_sum * jnp.concatenate([shift] * BASIS, axis=1)
    high = lhs.astype(BF16)
    low = (lhs - high.astype(F32)).astype(BF16)
    scaled = scaled_ref[...]
    return jnp.dot(high, scaled, preferred_element_type=F32) + jnp.dot(
        low, scaled, preferred_element_type=F32
    )


def first_kernel(
    local_mean_ref, a_ref, b_ref, gathered_ref, z_any, core_any, own_any, band_any, mix_any, gain_any, tap_sum_any,
    s_any, res_any, mid_ref, shift_ref, scaled_ref, sums_ref, new_mean_ref,
    res_ref, mix_ref, gain_ref, tap_sum_ref, edge_sum_ref, u_ref, edge_ref, z_ref, core_ref, own_ref, band_ref,
    s_ref, weight_ref, in_sems, out_sems,
):
    z_in, core_in, own_in = start_all(
        [(z_any, z_ref), (core_any, core_ref), (own_any, own_ref)], in_sems
    )
    pairs = (
        (band_any, band_ref),
        (mix_any.at[0], mix_ref),
        (gain_any, gain_ref),
        (tap_sum_any, tap_sum_ref),
    )
    later = [pltpu.make_async_copy(s, t, in_sems.at[3 + n]) for n, (s, t) in enumerate(pairs)]
    band_in, mix_in, gain_in, tap_in = later
    xh, core = lax.axis_index("xh"), lax.axis_index("core")
    local_mean = local_mean_ref[...]

    def put_row(r, from_z, own, from_core):
        from_z, own, from_core = from_z.astype(F32), own.astype(F32), from_core.astype(F32)
        left = jnp.where(core == 0, from_z, from_core)
        right = jnp.where(core == 0, from_core, from_z)
        pad = jnp.zeros((12, CHANS), F32)
        u_ref[r] = (jnp.concatenate([left, own, right, pad], axis=0) - local_mean).astype(BF16)
        res = jnp.concatenate([left[HMAX:], own, right[:HMAX], pad[:8]], axis=0)
        return res.astype(BF16)

    def own_row(i, _):
        res_ref[i + 1] = put_row(i + 2, z_ref[i], own_ref[i], core_ref[i])
        return 0

    z_in.wait()
    core_in.wait()
    own_in.wait()
    for fetch in later:
        fetch.start()
    lax.fori_loop(0, ROWS, own_row, 0)
    band_in.wait()

    def rim(piece, upper):
        use_b = (xh == 0) if upper else (xh == 1)
        return jnp.where(use_b, b_ref[piece].astype(F32), a_ref[piece].astype(F32))

    for upper in (True, False):
        for j in range(2):
            res = put_row(
                j if upper else ROWS + 2 + j, rim(j, upper), rim(2 + j, upper), rim(4 + j, upper)
            )
            if j == (1 if upper else 0):
                res_ref[0 if upper else ROWS + 1] = res
        place = 0 if upper else 1
        lines = rim(6, upper)[:, :128]
        for k in range(BASIS):

            def store(lanes, value):
                edge_ref[place, k * TILE : (k + 1) * TILE, lanes] = value

            rows = [spread(lines[3 * k + r : 3 * k + r + 1]) for r in range(3)]
            put_band(rows, place, store)
            whole = jnp.sum((rows[0] + rows[1] + rows[2])[0:1], axis=1, keepdims=True)
            edge_sum_ref[place : place + 1, k * CHANS : (k + 1) * CHANS] = jnp.broadcast_to(
                whole, (1, CHANS)
            )

    tiles = WIDE // TILE
    def one_pair(p, _):
        band = band_ref[pl.ds(2 * p - 1, 2)].reshape(2 * HIGH, 4 * SPAN)
        convolve(p, band, u_ref, s_ref, tiles)
        return 0

    convolve(0, jnp.concatenate([edge_ref[0], band_ref[0]], axis=0), u_ref, s_ref, tiles)
    lax.fori_loop(1, ROWS // 2, one_pair, 0)
    convolve(ROWS // 2, jnp.concatenate([band_ref[ROWS - 1], edge_ref[1]], axis=0), u_ref, s_ref, tiles)

    strips = [(pl.ds(1, ROWS), pl.ds(n * (WIDE - TILE), TILE)) for n in range(2)]
    strips += [(pl.ds(n * (ROWS + 1), 1),) for n in range(2)]
    rim = start_all([(s_ref.at[at], s_any.at[at]) for at in strips] + [(res_ref, res_any)], out_sems)
    mid = 4 * TILE
    parts = (11, 11)
    spans = [(sum(parts[:g]), parts[g]) for g in range(len(parts))]
    whole = area_weights(weight_ref)
    gain_in.wait()
    mix_in.wait()
    mean, column = scale_of(gathered_ref, gain_ref[0:1])
    shift = local_mean - mean
    scale_mixing(column, mix_ref, scaled_ref)
    tap_in.wait()
    shift_ref[0:ROWS] = shift_rows(tap_sum_ref[...], shift, scaled_ref)
    shift_ref[ROWS : ROWS + 2] = shift_rows(edge_sum_ref[...], shift, scaled_ref)
    column = lax.broadcasted_iota(jnp.int32, (mid, CHANS), 0) + TILE
    mine = (column >= HMAX) & (column < HMAX + COLS)
    first = second = jnp.zeros((mid, CHANS), F32)
    for at, n in spans:
        lhs = s_ref[at + 1 : at + 1 + n, TILE : TILE + mid].reshape(n * mid, DEEP)
        conv = jnp.dot(lhs, scaled_ref[...], preferred_element_type=F32).reshape(n, mid, CHANS)
        for i in range(at, at + n):
            grown = jax.nn.gelu(conv[i - at] + shift_ref[i : i + 1])
            new = (res_ref[i + 1, TILE : TILE + mid].astype(F32) + grown).astype(BF16)
            mid_ref[i] = new
            v = jnp.where(mine, new.astype(F32), 0.0)
            wv = weight_ref[i : i + 1] * v
            first, second = first + wv, second + wv * v
    first = jnp.sum(first, axis=0, keepdims=True)
    sums_ref[0:1] = first
    sums_ref[1:2] = jnp.sum(second, axis=0, keepdims=True)
    new_mean_ref[...] = first / whole
    for send in rim:
        send.wait()


def second_conv_kernel(
    mean_ref, shift_ref, mid_ref, scaled_ref, res_any, band_any, s_any, mix_any,
    out_any, mix_ref, res_ref, u_ref, s_ref, rows_ref, out_ref, band_ref, in_sems, out_sems,
):
    strips = [(pl.ds(1, ROWS), pl.ds(n * (WIDE - TILE), TILE)) for n in range(2)]
    edges = [n * (ROWS + 1) for n in range(2)]
    fetches = start_all(
        [(s_any.at[at], s_ref.at[n]) for n, at in enumerate(strips)]
        + [(s_any.at[at], rows_ref.at[n]) for n, at in enumerate(edges)]
        + [(res_any.at[at], res_ref.at[at]) for at in strips + edges],
        in_sems,
    )
    band_in = pltpu.make_async_copy(band_any, band_ref, in_sems.at[8])
    mix_in = pltpu.make_async_copy(mix_any.at[1], mix_ref, in_sems.at[9])
    local_mean = mean_ref[...]

    def mid_row(i, _):
        u_ref[i + 1, TILE : 5 * TILE] = (mid_ref[i].astype(F32) - local_mean).astype(BF16)
        return 0

    lax.fori_loop(0, ROWS, mid_row, 0)

    for fetch in fetches:
        fetch.wait()
    band_in.start()
    mix_in.start()
    for left in range(2):
        at = slice(left * (WIDE - TILE), left * (WIDE - TILE) + TILE)
        lhs = s_ref[left].reshape(ROWS * TILE, DEEP)
        conv = jnp.dot(lhs, scaled_ref[...], preferred_element_type=F32).reshape(ROWS, TILE, CHANS)
        for i in range(ROWS):
            grown = jax.nn.gelu(conv[i] + shift_ref[i : i + 1])
            new = (res_ref[i + 1, at].astype(F32) + grown).astype(BF16).astype(F32)
            u_ref[i + 1, at] = (new - local_mean).astype(BF16)
    lhs = rows_ref[...].reshape(2 * WIDE, DEEP)
    conv = jnp.dot(lhs, scaled_ref[...], preferred_element_type=F32).reshape(2, WIDE, CHANS)
    for n in range(2):
        e = n * (ROWS + 1)
        grown = jax.nn.gelu(conv[n] + shift_ref[ROWS + n : ROWS + n + 1])
        new = (res_ref[e].astype(F32) + grown).astype(BF16).astype(F32)
        u_ref[e] = (new - local_mean).astype(BF16)

    band_in.wait()

    def one_pair(p, _):
        band = band_ref[pl.ds(2 * p, 2)].reshape(2 * HIGH, 4 * SPAN)
        convolve(p, band, u_ref, out_ref, 3)
        send(p).start()
        return 0

    def send(p):
        at = pl.ds(2 * p, 2)
        return pltpu.make_async_copy(out_ref.at[at], out_any.at[at], out_sems.at[p])

    def end(p, _):
        send(p).wait()
        return 0

    lax.fori_loop(0, ROWS // 2, one_pair, 0)
    lax.fori_loop(0, ROWS // 2, end, 0)
    mix_in.wait()


def second_mix_kernel(
    gathered_ref, local_mean_ref, mix_ref, mid_ref, gain_any, s_any, tap_sum_any, out_any,
    gain_ref, s_ref, tap_sum_ref, scaled_ref, shift_ref, out_ref, in_sems, out_sems,
):
    cols = 3 * TILE
    parts = (4, 8, 10)
    spans = [(sum(parts[:g]), parts[g]) for g in range(len(parts))]
    gain_in, tap_in, *s_in = start_all(
        [(gain_any, gain_ref), (tap_sum_any, tap_sum_ref)]
        + [(s_any.at[pl.ds(at, n)], s_ref.at[pl.ds(at, n)]) for at, n in spans],
        in_sems,
    )
    gain_in.wait()
    mean, column = scale_of(gathered_ref, gain_ref[1:2])
    shift = local_mean_ref[...] - mean
    scale_mixing(column, mix_ref, scaled_ref)
    tap_in.wait()
    shift_ref[...] = shift_rows(tap_sum_ref[...], shift, scaled_ref)
    sends = []
    for g, (at, n) in enumerate(spans):
        s_in[g].wait()
        lhs = s_ref[at : at + n].reshape(n * cols, DEEP)
        conv = jnp.dot(lhs, scaled_ref[...], preferred_element_type=F32).reshape(n, cols, CHANS)
        for i in range(at, at + n):
            grown = jax.nn.gelu(conv[i - at] + shift_ref[i : i + 1])
            res = mid_ref[i].astype(F32)[HMAX - TILE : HMAX - TILE + COLS]
            out_ref[i] = (res + grown[:COLS]).astype(BF16)
        span = pl.ds(at, n)
        sends.append(pltpu.make_async_copy(out_ref.at[span], out_any.at[span], out_sems.at[g]))
        sends[-1].start()
    for send in sends:
        send.wait()


def shape(*dims, dtype=BF16):
    return jax.ShapeDtypeStruct(dims, dtype)


SMEM = pl.BlockSpec(memory_space=pltpu.SMEM)
VMEM = pl.BlockSpec(memory_space=pltpu.VMEM)
HBM = pl.BlockSpec(memory_space=pltpu.HBM)
KEPT = pl.BlockSpec(memory_space=pltpu.VMEM)


def call(kernel, ins, outs, scratch=(), flops=10**6):
    def out_shape(o, spec):
        space = {id(HBM): pltpu.HBM, id(KEPT): pltpu.VMEM}.get(id(spec))
        return o if space is None else space(o.shape, o.dtype)

    run = pl.pallas_call(
        kernel,
        out_shape=[out_shape(*o) for o in outs],
        in_specs=ins,
        out_specs=[spec for _, spec in outs],
        scratch_shapes=list(scratch),
        compiler_params=pltpu.CompilerParams(vmem_limit_bytes=VMEM_LIMIT),
        cost_estimate=pl.CostEstimate(flops=flops, bytes_accessed=10**6, transcendentals=0),
    )

    def in_place(v, spec):
        space = {id(HBM): pltpu.HBM, id(KEPT): pltpu.VMEM}.get(id(spec))
        return v if space is None else pltpu.with_memory_space_constraint(v, space)

    return lambda *values: run(*[in_place(v, spec) for v, spec in zip(values, ins)])


def swap_pairs(count, first):
    pairs = []
    for i in range(first, count - 1, 2):
        pairs += [(i, i + 1), (i + 1, i)]
    return pairs


def from_other_core(v):
    return lax.ppermute(v, "core", [(0, 1), (1, 0)])


def gather(both):
    return lax.all_to_all(both, ("y", "xh", "z"), 0, 0)


def buffer(*dims):
    return pltpu.VMEM(dims, BF16)


def semaphores(count):
    return pltpu.SemaphoreType.DMA((count,))


def floats(*dims):
    return pltpu.VMEM(dims, F32)


def local(x, norm_gain, mixing, kernel_psi, lon_reach):
    peers = lax.axis_size("y") * lax.axis_size("xh") * lax.axis_size("z")
    sums_out = (shape(2, CHANS, dtype=F32), VMEM)
    mean_out = (shape(1, CHANS, dtype=F32), VMEM)
    both_out = (shape(peers, 2, CHANS, dtype=F32), VMEM)
    tap_sum_out = (shape(ROWS, DEEP, dtype=F32), HBM)
    mid_cols, own_cols = 4 * TILE, 3 * TILE

    from_core = from_other_core(x)
    ring = []
    for z in range(8):
        a, b = 2 * z + 1, (2 * z + 2) % 16
        ring += [(a, b), (b, a)]
    from_z = lax.ppermute(x, LON, ring)

    psi = jnp.transpose(kernel_psi, (1, 2, 3, 0, 4))
    band_outs = [(shape(ROWS, HIGH, 4 * SPAN), HBM), tap_sum_out]
    edge_out = (shape(2, 3 * BASIS, 128, dtype=F32), VMEM)
    sums, mean, edge = call(
        sums_kernel,
        [HBM, HBM, HBM],
        [sums_out, mean_out, edge_out],
        [
            buffer(ROWS, COLS, CHANS),
            pltpu.SMEM((ROWS,), jnp.int32),
            buffer(BASIS, 2, 3, BLOCKS, TAPS),
            floats(24, CHANS),
            semaphores(5),
        ],
    )(x, lon_reach, psi)
    (both,) = call(add_kernel, [VMEM, VMEM], [both_out])(sums, from_other_core(sums))
    gathered = gather(both)

    message = (shape(7, COLS, CHANS), VMEM)
    to_a, to_b = call(message_kernel, [VMEM, HBM] + [VMEM] * 3, [message, message], [semaphores(2)])(
        from_z, x, from_core, edge, both
    )
    band1, tap_sum1, band2, tap_sum2 = call(
        prep_kernel,
        [VMEM, HBM, HBM],
        band_outs + band_outs,
        [pltpu.SMEM((ROWS,), jnp.int32), buffer(BASIS, ROWS, 3, BLOCKS, TAPS)]
        + [buffer(ROWS, HIGH, 4 * SPAN), floats(ROWS, DEEP)] * 2
        + [floats(BASIS, ROWS, 128), semaphores(9)],
        flops=5 * 10**9,
    )(to_a, lon_reach, psi)
    got_a = lax.ppermute(to_a, LAT, swap_pairs(8, 0))
    got_b = lax.ppermute(to_b, LAT, swap_pairs(8, 1))

    s1, res, mid, shift, scaled, sums1, mean1 = call(
        first_kernel,
        [VMEM] * 4 + [HBM] * 7,
        [
            (shape(ROWS + 2, WIDE, DEEP), HBM),
            (shape(ROWS + 2, WIDE, CHANS), HBM),
            (shape(ROWS, mid_cols, CHANS), KEPT),
            (shape(ROWS + 2, CHANS, dtype=F32), KEPT),
            (shape(DEEP, CHANS), KEPT),
            sums_out,
            mean_out,
        ],
        [
            buffer(ROWS + 2, WIDE, CHANS),
            buffer(BASIS, CHANS, CHANS),
            floats(BLOCKS, CHANS),
            floats(ROWS, DEEP),
            floats(2, DEEP),
            buffer(ROWS + 4, 144, CHANS),
            buffer(2, HIGH, 4 * SPAN),
            buffer(ROWS, COLS, CHANS),
            buffer(ROWS, COLS, CHANS),
            buffer(ROWS, COLS, CHANS),
            buffer(ROWS, HIGH, 4 * SPAN),
            buffer(ROWS + 2, WIDE, DEEP),
            floats(24, CHANS),
            semaphores(7),
            semaphores(5),
        ],
    )(mean, got_a, got_b, gathered, from_z, from_core, x, band1, mixing, norm_gain, tap_sum1)
    (both1,) = call(add_kernel, [VMEM, VMEM], [both_out])(sums1, from_other_core(sums1))
    gathered1 = gather(both1)
    s2, mix2 = call(
        second_conv_kernel,
        [VMEM] + [KEPT] * 3 + [HBM] * 4,
        [(shape(ROWS, own_cols, DEEP), HBM), (shape(BASIS, CHANS, CHANS), KEPT)],
        [
            buffer(ROWS + 2, WIDE, CHANS),
            buffer(ROWS + 2, WIDE, CHANS),
            buffer(2, ROWS, TILE, DEEP),
            buffer(2, WIDE, DEEP),
            buffer(ROWS, own_cols, DEEP),
            buffer(ROWS, HIGH, 4 * SPAN),
            semaphores(10),
            semaphores(11),
        ],
        flops=9 * 10**9,
    )(mean1, shift, mid, scaled, res, band2, s1, mixing)
    (out,) = call(
        second_mix_kernel,
        [VMEM] * 2 + [KEPT] * 2 + [HBM] * 3,
        [(shape(ROWS, COLS, CHANS), HBM)],
        [
            floats(BLOCKS, CHANS),
            buffer(ROWS, own_cols, DEEP),
            floats(ROWS, DEEP),
            buffer(DEEP, CHANS),
            floats(ROWS, CHANS),
            buffer(ROWS, COLS, CHANS),
            semaphores(5),
            semaphores(3),
        ],
        flops=2 * 10**9,
    )(gathered1, mean1, mix2, mid, norm_gain, s2, tap_sum2)
    return out


def solution(mesh):
    split = Mesh(mesh.devices.reshape(2, 4, 2, 8, 2), ("mem", "y", "xh", "z", "core"))
    placed = (P(LAT, LON, "mem"), P(), P(), P(None, None, LAT, None, None), P(LAT))
    return jax.shard_map(
        local, mesh=split, in_specs=placed, out_specs=P(LAT, LON, "mem"), check_vma=False
    )
```

```python
import functools
import math

import jax
import jax.numpy as jnp
import numpy as np
from jax import lax
from jax.experimental import pallas as pl
from jax.experimental.pallas import tpu as pltpu
from jax.sharding import Mesh, PartitionSpec as P

BLOCKS = 2
HMAX = 22
TAPS = 2 * HMAX + 1
TILE = 16
SPAN = 64
ROWS = 22
COLS = 44
CHANS = 256
BASIS = 9
N_LAT = 176
N_LON = 704
WIDE = 96
DEEP = BASIS * CHANS
HIGH = BASIS * TILE
LAT = ("y", "xh")
LON = ("z", "core")
F32 = jnp.float32
BF16 = jnp.bfloat16
VMEM_LIMIT = 28 * 1024 * 1024
WEIGHTS = np.cos(np.pi * (np.arange(N_LAT) + 0.5) / N_LAT - np.pi / 2)
TOTAL = float(N_LON * WEIGHTS.sum())


def lat_index():
    return lax.axis_index("y") * 2 + lax.axis_index("xh")


def area_weights(weight_ref):
    row = lax.broadcasted_iota(jnp.int32, (24, CHANS), 0)
    angle = ((lat_index() * ROWS + row).astype(F32) + 0.5) * (math.pi / N_LAT)
    weight = jnp.where(row < ROWS, jnp.sin(angle), 0.0)
    weight_ref[...] = weight
    return COLS * jnp.sum(weight, axis=0, keepdims=True)


def start_all(pairs, sems):
    copies = [pltpu.make_async_copy(s, t, sems.at[n]) for n, (s, t) in enumerate(pairs)]
    for copy in copies:
        copy.start()
    return copies


def put_band(rows, odd, store):
    halves = [None, None]
    for r in range(3):
        place = r + odd
        moved = pltpu.roll(rows[r], SPAN * (place % 2), 1, stride=1, stride_axis=0)
        half = place // 2
        halves[half] = moved if halves[half] is None else halves[half] + moved
    store(slice(0, 128), halves[0].astype(BF16))
    store(slice(128, 256), halves[1].astype(BF16))


def spread(line):
    return jnp.broadcast_to(line, (TILE, 128))


def taps_of(reach_ref, psi_ref, block, i, k, at=None):
    tap = lax.broadcasted_iota(jnp.int32, (1, TAPS), 1) - HMAX
    rest = jnp.zeros((1, 128 - TAPS), F32)
    near = jnp.abs(tap) <= reach_ref[i]
    row = lat_index() * ROWS + i - 1
    taps = []
    for r in range(3):
        keep = near & (row + r >= 0) & (row + r < N_LAT)
        line = jnp.where(keep, psi_ref[k, i if at is None else at, r].astype(F32)[block : block + 1], 0.0)
        taps.append(jnp.broadcast_to(jnp.concatenate([line, rest], axis=1), (TILE, 128)))
    return taps


def make_bands(reach_ref, psi_ref, block, band_ref, tap_sum_ref, line_ref, sends):
    def two_rows(p, _):
        for n in range(2):
            i = 2 * p + n
            for k in range(BASIS):

                def store(lanes, value):
                    band_ref[i, k * TILE : (k + 1) * TILE, lanes] = value

                rows = taps_of(reach_ref, psi_ref, block, i, k)
                put_band(rows, (n + 1 - block) % 2, store)
                line_ref[k, pl.ds(i, 1)] = (rows[0] + rows[1] + rows[2])[0:1]
        return 0

    lax.fori_loop(0, 6, two_rows, 0)
    sends[0].start()
    lax.fori_loop(6, ROWS // 2, two_rows, 0)
    sends[1].start()
    for k in range(BASIS):
        whole = jnp.sum(line_ref[k], axis=1, keepdims=True)
        tap_sum_ref[:, k * CHANS : (k + 1) * CHANS] = jnp.broadcast_to(whole, (ROWS, CHANS))


def sums_kernel(
    x_any, reach_any, psi_any, sums_ref, mean_ref, edge_ref, x_ref, reach_ref, psi_ref, weight_ref, sems
):
    ends = (0, ROWS - 1)
    reach_in, *psi_in = [
        pltpu.make_async_copy(s, t, sems.at[2 + n])
        for n, (s, t) in enumerate(
            [(reach_any, reach_ref)] + [(psi_any.at[:, i], psi_ref.at[:, n]) for n, i in enumerate(ends)]
        )
    ]
    for fetch in (reach_in, *psi_in):
        fetch.start()
    half = ROWS // 2
    parts = start_all([(x_any.at[pl.ds(n * half, half)], x_ref.at[pl.ds(n * half, half)]) for n in range(2)], sems)
    whole = area_weights(weight_ref)

    def add_row(i, carry):
        first, second = carry
        v = x_ref[i].astype(F32)
        wv = weight_ref[pl.ds(i, 1)] * v
        return first + wv, second + wv * v

    zero = jnp.zeros((COLS, CHANS), F32)
    parts[0].wait()
    carry = lax.fori_loop(0, half, add_row, (zero, zero))
    parts[1].wait()
    first, second = lax.fori_loop(half, ROWS, add_row, carry)
    first = jnp.sum(first, axis=0, keepdims=True)
    sums_ref[0:1] = first
    sums_ref[1:2] = jnp.sum(second, axis=0, keepdims=True)
    mean_ref[...] = first / whole
    for fetch in (reach_in, *psi_in):
        fetch.wait()
    for n, i in enumerate(ends):
        for k in range(BASIS):
            taps = taps_of(reach_ref, psi_ref, 0, i, k, n)
            for r in range(3):
                edge_ref[n, 3 * k + r : 3 * k + r + 1] = taps[r][0:1]


def prep_kernel(
    message_ref, reach_any, psi_any, band1_any, tap_sum1_any, band2_any, tap_sum2_any,
    reach_ref, psi_ref, band1_ref, tap_sum1_ref, band2_ref, tap_sum2_ref, line_ref, sems,
):
    psi_in, reach_in = start_all([(psi_any, psi_ref), (reach_any, reach_ref)], sems)
    psi_in.wait()
    reach_in.wait()
    outs = ((band1_ref, band1_any, tap_sum1_ref, tap_sum1_any), (band2_ref, band2_any, tap_sum2_ref, tap_sum2_any))
    half = ROWS // 2
    sends = []
    for block, (band_ref, band_any, tap_sum_ref, tap_sum_any) in enumerate(outs):
        pairs = [(band_ref.at[pl.ds(n * half, half)], band_any.at[pl.ds(n * half, half)]) for n in range(2)]
        pairs.append((tap_sum_ref, tap_sum_any))
        mine = [pltpu.make_async_copy(*pair, sems.at[3 + 3 * block + n]) for n, pair in enumerate(pairs)]
        make_bands(reach_ref, psi_ref, block, band_ref, tap_sum_ref, line_ref, mine)
        mine[2].start()
        sends += mine
    for send in sends:
        send.wait()


def message_kernel(z_ref, own_any, core_ref, edge_ref, both_ref, a_ref, b_ref, sems):
    xh = lax.axis_index("xh")
    starts = [jnp.where(xh == n, ROWS - 2, 0) for n in range(2)]
    copies = start_all(
        [(own_any.at[pl.ds(s, 2)], out.at[pl.ds(2, 2)]) for s, out in zip(starts, (a_ref, b_ref))], sems
    )
    for n, out in enumerate((a_ref, b_ref)):
        taps = jnp.where(xh == n, edge_ref[1], edge_ref[0])
        out[0:2] = z_ref[pl.ds(starts[n], 2)]
        out[4:6] = core_ref[pl.ds(starts[n], 2)]
        out[6] = jnp.zeros((COLS, CHANS), BF16)
        out[6, 0:32, 0:128] = jnp.concatenate([taps, jnp.zeros((5, 128), F32)], axis=0).astype(BF16)
    for copy in copies:
        copy.wait()


def add_kernel(sums_ref, other_ref, both_ref):
    both_ref[...] = jnp.broadcast_to((sums_ref[...] + other_ref[...])[None], both_ref.shape)


def convolve(p, band, u_ref, s_ref, tiles):
    for t in range(tiles):
        window = u_ref[pl.ds(2 * p, 4), TILE * t : TILE * t + SPAN, :].reshape(4 * SPAN, CHANS)
        s = jnp.dot(band, window, preferred_element_type=F32).astype(BF16)
        for ri in range(2):
            for k in range(BASIS):
                at = (ri * BASIS + k) * TILE
                s_ref[2 * p + ri, TILE * t : TILE * t + TILE, k * CHANS : (k + 1) * CHANS] = s[
                    at : at + TILE
                ]


def scale_of(gathered_ref, gain):
    total = jnp.sum(gathered_ref[...], axis=0)
    mean = total[0:1] / TOTAL
    scale = lax.rsqrt(total[1:2] / TOTAL - mean * mean + 1e-05) * gain
    diagonal = lax.broadcasted_iota(jnp.int32, (CHANS, CHANS), 0) == lax.broadcasted_iota(
        jnp.int32, (CHANS, CHANS), 1
    )
    return mean, jnp.sum(jnp.where(diagonal, scale, 0.0), axis=1, keepdims=True)


def scale_mixing(column, mix_ref, scaled_ref):
    for k in range(BASIS):
        scaled_ref[k * CHANS : (k + 1) * CHANS] = (mix_ref[k].astype(F32) * column).astype(BF16)


def shift_rows(tap_sum, shift, scaled_ref):
    lhs = tap_sum * jnp.concatenate([shift] * BASIS, axis=1)
    high = lhs.astype(BF16)
    low = (lhs - high.astype(F32)).astype(BF16)
    scaled = scaled_ref[...]
    return jnp.dot(high, scaled, preferred_element_type=F32) + jnp.dot(
        low, scaled, preferred_element_type=F32
    )


def first_kernel(
    local_mean_ref, a_ref, b_ref, gathered_ref, z_any, core_any, own_any, band_any, mix_any, gain_any, tap_sum_any,
    s_any, res_any, mid_ref, shift_ref, scaled_any, sums_ref, new_mean_ref,
    res_ref, mix_ref, gain_ref, tap_sum_ref, edge_sum_ref, u_ref, edge_ref, z_ref, core_ref, own_ref, band_ref,
    s_ref, scaled_ref, weight_ref, in_sems, out_sems,
):
    z_in, core_in, own_in, band_in, mix_in, gain_in, tap_in = start_all(
        [
            (z_any, z_ref),
            (core_any, core_ref),
            (own_any, own_ref),
            (band_any, band_ref),
            (mix_any.at[0], mix_ref),
            (gain_any, gain_ref),
            (tap_sum_any, tap_sum_ref),
        ],
        in_sems,
    )
    xh, core = lax.axis_index("xh"), lax.axis_index("core")
    local_mean = local_mean_ref[...]

    def put_row(r, from_z, own, from_core):
        from_z, own, from_core = from_z.astype(F32), own.astype(F32), from_core.astype(F32)
        left = jnp.where(core == 0, from_z, from_core)
        right = jnp.where(core == 0, from_core, from_z)
        pad = jnp.zeros((12, CHANS), F32)
        u_ref[r] = (jnp.concatenate([left, own, right, pad], axis=0) - local_mean).astype(BF16)
        res = jnp.concatenate([left[HMAX:], own, right[:HMAX], pad[:8]], axis=0)
        return res.astype(BF16)

    def own_row(i, _):
        res_ref[i + 1] = put_row(i + 2, z_ref[i], own_ref[i], core_ref[i])
        return 0

    z_in.wait()
    core_in.wait()
    own_in.wait()
    lax.fori_loop(0, ROWS, own_row, 0)
    band_in.wait()

    def rim(piece, upper):
        use_b = (xh == 0) if upper else (xh == 1)
        return jnp.where(use_b, b_ref[piece].astype(F32), a_ref[piece].astype(F32))

    for upper in (True, False):
        for j in range(2):
            res = put_row(
                j if upper else ROWS + 2 + j, rim(j, upper), rim(2 + j, upper), rim(4 + j, upper)
            )
            if j == (1 if upper else 0):
                res_ref[0 if upper else ROWS + 1] = res
        place = 0 if upper else 1
        lines = rim(6, upper)[:, :128]
        for k in range(BASIS):

            def store(lanes, value):
                edge_ref[place, k * TILE : (k + 1) * TILE, lanes] = value

            rows = [spread(lines[3 * k + r : 3 * k + r + 1]) for r in range(3)]
            put_band(rows, place, store)
            whole = jnp.sum((rows[0] + rows[1] + rows[2])[0:1], axis=1, keepdims=True)
            edge_sum_ref[place : place + 1, k * CHANS : (k + 1) * CHANS] = jnp.broadcast_to(
                whole, (1, CHANS)
            )

    tiles = WIDE // TILE
    def one_pair(p, _):
        band = band_ref[pl.ds(2 * p - 1, 2)].reshape(2 * HIGH, 4 * SPAN)
        convolve(p, band, u_ref, s_ref, tiles)
        return 0

    convolve(0, jnp.concatenate([edge_ref[0], band_ref[0]], axis=0), u_ref, s_ref, tiles)
    lax.fori_loop(1, ROWS // 2, one_pair, 0)
    convolve(ROWS // 2, jnp.concatenate([band_ref[ROWS - 1], edge_ref[1]], axis=0), u_ref, s_ref, tiles)

    strips = [(pl.ds(1, ROWS), pl.ds(n * (WIDE - TILE), TILE)) for n in range(2)]
    strips += [(pl.ds(n * (ROWS + 1), 1),) for n in range(2)]
    rim = start_all([(s_ref.at[at], s_any.at[at]) for at in strips] + [(res_ref, res_any)], out_sems)
    mid = 4 * TILE
    parts = (11, 11)
    spans = [(sum(parts[:g]), parts[g]) for g in range(len(parts))]
    whole = area_weights(weight_ref)
    gain_in.wait()
    mix_in.wait()
    mean, column = scale_of(gathered_ref, gain_ref[0:1])
    shift = local_mean - mean
    scale_mixing(column, mix_ref, scaled_ref)
    send_scaled = pltpu.make_async_copy(scaled_ref, scaled_any, out_sems.at[5])
    send_scaled.start()
    tap_in.wait()
    shift_ref[0:ROWS] = shift_rows(tap_sum_ref[...], shift, scaled_ref)
    shift_ref[ROWS : ROWS + 2] = shift_rows(edge_sum_ref[...], shift, scaled_ref)
    column = lax.broadcasted_iota(jnp.int32, (mid, CHANS), 0) + TILE
    mine = (column >= HMAX) & (column < HMAX + COLS)
    first = second = jnp.zeros((mid, CHANS), F32)
    for at, n in spans:
        lhs = s_ref[at + 1 : at + 1 + n, TILE : TILE + mid].reshape(n * mid, DEEP)
        conv = jnp.dot(lhs, scaled_ref[...], preferred_element_type=F32).reshape(n, mid, CHANS)
        for i in range(at, at + n):
            grown = jax.nn.gelu(conv[i - at] + shift_ref[i : i + 1])
            new = (res_ref[i + 1, TILE : TILE + mid].astype(F32) + grown).astype(BF16)
            mid_ref[i] = new
            v = jnp.where(mine, new.astype(F32), 0.0)
            wv = weight_ref[i : i + 1] * v
            first, second = first + wv, second + wv * v
    first = jnp.sum(first, axis=0, keepdims=True)
    sums_ref[0:1] = first
    sums_ref[1:2] = jnp.sum(second, axis=0, keepdims=True)
    new_mean_ref[...] = first / whole
    send_scaled.wait()
    for send in rim:
        send.wait()


def second_conv_kernel(
    mean_ref, shift_ref, mid_ref, res_any, band_any, scaled_any, s_any, mix_any,
    out_any, mix_ref, res_ref, u_ref, s_ref, rows_ref, out_ref, scaled_ref, band_ref, in_sems, out_sems,
):
    strips = [(pl.ds(1, ROWS), pl.ds(n * (WIDE - TILE), TILE)) for n in range(2)]
    edges = [n * (ROWS + 1) for n in range(2)]
    fetches = start_all(
        [(scaled_any, scaled_ref)]
        + [(s_any.at[at], s_ref.at[n]) for n, at in enumerate(strips)]
        + [(s_any.at[at], rows_ref.at[n]) for n, at in enumerate(edges)]
        + [(res_any.at[at], res_ref.at[at]) for at in strips + edges],
        in_sems,
    )
    band_in = pltpu.make_async_copy(band_any, band_ref, in_sems.at[9])
    mix_in = pltpu.make_async_copy(mix_any.at[1], mix_ref, in_sems.at[10])
    local_mean = mean_ref[...]

    def mid_row(i, _):
        u_ref[i + 1, TILE : 5 * TILE] = (mid_ref[i].astype(F32) - local_mean).astype(BF16)
        return 0

    lax.fori_loop(0, ROWS, mid_row, 0)

    for fetch in fetches:
        fetch.wait()
    band_in.start()
    mix_in.start()
    for left in range(2):
        at = slice(left * (WIDE - TILE), left * (WIDE - TILE) + TILE)
        lhs = s_ref[left].reshape(ROWS * TILE, DEEP)
        conv = jnp.dot(lhs, scaled_ref[...], preferred_element_type=F32).reshape(ROWS, TILE, CHANS)
        for i in range(ROWS):
            grown = jax.nn.gelu(conv[i] + shift_ref[i : i + 1])
            new = (res_ref[i + 1, at].astype(F32) + grown).astype(BF16).astype(F32)
            u_ref[i + 1, at] = (new - local_mean).astype(BF16)
    lhs = rows_ref[...].reshape(2 * WIDE, DEEP)
    conv = jnp.dot(lhs, scaled_ref[...], preferred_element_type=F32).reshape(2, WIDE, CHANS)
    for n in range(2):
        e = n * (ROWS + 1)
        grown = jax.nn.gelu(conv[n] + shift_ref[ROWS + n : ROWS + n + 1])
        new = (res_ref[e].astype(F32) + grown).astype(BF16).astype(F32)
        u_ref[e] = (new - local_mean).astype(BF16)

    band_in.wait()

    def one_pair(p, _):
        band = band_ref[pl.ds(2 * p, 2)].reshape(2 * HIGH, 4 * SPAN)
        convolve(p, band, u_ref, out_ref, 3)
        send(p).start()
        return 0

    def send(p):
        at = pl.ds(2 * p, 2)
        return pltpu.make_async_copy(out_ref.at[at], out_any.at[at], out_sems.at[p])

    def end(p, _):
        send(p).wait()
        return 0

    lax.fori_loop(0, ROWS // 2, one_pair, 0)
    lax.fori_loop(0, ROWS // 2, end, 0)
    mix_in.wait()


def second_mix_kernel(
    gathered_ref, local_mean_ref, mix_ref, mid_ref, gain_any, s_any, tap_sum_any, out_any,
    gain_ref, s_ref, tap_sum_ref, scaled_ref, shift_ref, out_ref, in_sems, out_sems,
):
    cols = 3 * TILE
    parts = (4, 8, 10)
    spans = [(sum(parts[:g]), parts[g]) for g in range(len(parts))]
    gain_in, tap_in, *s_in = start_all(
        [(gain_any, gain_ref), (tap_sum_any, tap_sum_ref)]
        + [(s_any.at[pl.ds(at, n)], s_ref.at[pl.ds(at, n)]) for at, n in spans],
        in_sems,
    )
    gain_in.wait()
    mean, column = scale_of(gathered_ref, gain_ref[1:2])
    shift = local_mean_ref[...] - mean
    scale_mixing(column, mix_ref, scaled_ref)
    tap_in.wait()
    shift_ref[...] = shift_rows(tap_sum_ref[...], shift, scaled_ref)
    sends = []
    for g, (at, n) in enumerate(spans):
        s_in[g].wait()
        lhs = s_ref[at : at + n].reshape(n * cols, DEEP)
        conv = jnp.dot(lhs, scaled_ref[...], preferred_element_type=F32).reshape(n, cols, CHANS)
        for i in range(at, at + n):
            grown = jax.nn.gelu(conv[i - at] + shift_ref[i : i + 1])
            res = mid_ref[i].astype(F32)[HMAX - TILE : HMAX - TILE + COLS]
            out_ref[i] = (res + grown[:COLS]).astype(BF16)
        span = pl.ds(at, n)
        sends.append(pltpu.make_async_copy(out_ref.at[span], out_any.at[span], out_sems.at[g]))
        sends[-1].start()
    for send in sends:
        send.wait()


def shape(*dims, dtype=BF16):
    return jax.ShapeDtypeStruct(dims, dtype)


SMEM = pl.BlockSpec(memory_space=pltpu.SMEM)
VMEM = pl.BlockSpec(memory_space=pltpu.VMEM)
HBM = pl.BlockSpec(memory_space=pltpu.HBM)
KEPT = pl.BlockSpec(memory_space=pltpu.VMEM)


def call(kernel, ins, outs, scratch=(), flops=10**6):
    def out_shape(o, spec):
        space = {id(HBM): pltpu.HBM, id(KEPT): pltpu.VMEM}.get(id(spec))
        return o if space is None else space(o.shape, o.dtype)

    run = pl.pallas_call(
        kernel,
        out_shape=[out_shape(*o) for o in outs],
        in_specs=ins,
        out_specs=[spec for _, spec in outs],
        scratch_shapes=list(scratch),
        compiler_params=pltpu.CompilerParams(vmem_limit_bytes=VMEM_LIMIT),
        cost_estimate=pl.CostEstimate(flops=flops, bytes_accessed=10**6, transcendentals=0),
    )

    def in_place(v, spec):
        space = {id(HBM): pltpu.HBM, id(KEPT): pltpu.VMEM}.get(id(spec))
        return v if space is None else pltpu.with_memory_space_constraint(v, space)

    return lambda *values: run(*[in_place(v, spec) for v, spec in zip(values, ins)])


def swap_pairs(count, first):
    pairs = []
    for i in range(first, count - 1, 2):
        pairs += [(i, i + 1), (i + 1, i)]
    return pairs


def from_other_core(v):
    return lax.ppermute(v, "core", [(0, 1), (1, 0)])


def gather(both):
    return lax.all_to_all(both, ("y", "xh", "z"), 0, 0)


def buffer(*dims):
    return pltpu.VMEM(dims, BF16)


def semaphores(count):
    return pltpu.SemaphoreType.DMA((count,))


def floats(*dims):
    return pltpu.VMEM(dims, F32)


def local(x, norm_gain, mixing, kernel_psi, lon_reach):
    peers = lax.axis_size("y") * lax.axis_size("xh") * lax.axis_size("z")
    sums_out = (shape(2, CHANS, dtype=F32), VMEM)
    mean_out = (shape(1, CHANS, dtype=F32), VMEM)
    both_out = (shape(peers, 2, CHANS, dtype=F32), VMEM)
    tap_sum_out = (shape(ROWS, DEEP, dtype=F32), HBM)
    mid_cols, own_cols = 4 * TILE, 3 * TILE

    from_core = from_other_core(x)
    ring = []
    for z in range(8):
        a, b = 2 * z + 1, (2 * z + 2) % 16
        ring += [(a, b), (b, a)]
    from_z = lax.ppermute(x, LON, ring)

    psi = jnp.transpose(kernel_psi, (1, 2, 3, 0, 4))
    band_outs = [(shape(ROWS, HIGH, 4 * SPAN), HBM), tap_sum_out]
    edge_out = (shape(2, 3 * BASIS, 128, dtype=F32), VMEM)
    sums, mean, edge = call(
        sums_kernel,
        [HBM, HBM, HBM],
        [sums_out, mean_out, edge_out],
        [
            buffer(ROWS, COLS, CHANS),
            pltpu.SMEM((ROWS,), jnp.int32),
            buffer(BASIS, 2, 3, BLOCKS, TAPS),
            floats(24, CHANS),
            semaphores(5),
        ],
    )(x, lon_reach, psi)
    (both,) = call(add_kernel, [VMEM, VMEM], [both_out])(sums, from_other_core(sums))
    gathered = gather(both)

    message = (shape(7, COLS, CHANS), VMEM)
    to_a, to_b = call(message_kernel, [VMEM, HBM] + [VMEM] * 3, [message, message], [semaphores(2)])(
        from_z, x, from_core, edge, both
    )
    band1, tap_sum1, band2, tap_sum2 = call(
        prep_kernel,
        [VMEM, HBM, HBM],
        band_outs + band_outs,
        [pltpu.SMEM((ROWS,), jnp.int32), buffer(BASIS, ROWS, 3, BLOCKS, TAPS)]
        + [buffer(ROWS, HIGH, 4 * SPAN), floats(ROWS, DEEP)] * 2
        + [floats(BASIS, ROWS, 128), semaphores(9)],
        flops=5 * 10**9,
    )(to_a, lon_reach, psi)
    got_a = lax.ppermute(to_a, LAT, swap_pairs(8, 0))
    got_b = lax.ppermute(to_b, LAT, swap_pairs(8, 1))

    s1, res, mid, shift, scaled, sums1, mean1 = call(
        first_kernel,
        [VMEM] * 4 + [HBM] * 7,
        [
            (shape(ROWS + 2, WIDE, DEEP), HBM),
            (shape(ROWS + 2, WIDE, CHANS), HBM),
            (shape(ROWS, mid_cols, CHANS), KEPT),
            (shape(ROWS + 2, CHANS, dtype=F32), KEPT),
            (shape(DEEP, CHANS), HBM),
            sums_out,
            mean_out,
        ],
        [
            buffer(ROWS + 2, WIDE, CHANS),
            buffer(BASIS, CHANS, CHANS),
            floats(BLOCKS, CHANS),
            floats(ROWS, DEEP),
            floats(2, DEEP),
            buffer(ROWS + 4, 144, CHANS),
            buffer(2, HIGH, 4 * SPAN),
            buffer(ROWS, COLS, CHANS),
            buffer(ROWS, COLS, CHANS),
            buffer(ROWS, COLS, CHANS),
            buffer(ROWS, HIGH, 4 * SPAN),
            buffer(ROWS + 2, WIDE, DEEP),
            buffer(DEEP, CHANS),
            floats(24, CHANS),
            semaphores(7),
            semaphores(6),
        ],
    )(mean, got_a, got_b, gathered, from_z, from_core, x, band1, mixing, norm_gain, tap_sum1)
    (both1,) = call(add_kernel, [VMEM, VMEM], [both_out])(sums1, from_other_core(sums1))
    gathered1 = gather(both1)
    s2, mix2 = call(
        second_conv_kernel,
        [VMEM] + [KEPT] * 2 + [HBM] * 5,
        [(shape(ROWS, own_cols, DEEP), HBM), (shape(BASIS, CHANS, CHANS), KEPT)],
        [
            buffer(ROWS + 2, WIDE, CHANS),
            buffer(ROWS + 2, WIDE, CHANS),
            buffer(2, ROWS, TILE, DEEP),
            buffer(2, WIDE, DEEP),
            buffer(ROWS, own_cols, DEEP),
            buffer(DEEP, CHANS),
            buffer(ROWS, HIGH, 4 * SPAN),
            semaphores(11),
            semaphores(11),
        ],
        flops=9 * 10**9,
    )(mean1, shift, mid, res, band2, scaled, s1, mixing)
    (out,) = call(
        second_mix_kernel,
        [VMEM] * 2 + [KEPT] * 2 + [HBM] * 3,
        [(shape(ROWS, COLS, CHANS), HBM)],
        [
            floats(BLOCKS, CHANS),
            buffer(ROWS, own_cols, DEEP),
            floats(ROWS, DEEP),
            buffer(DEEP, CHANS),
            floats(ROWS, CHANS),
            buffer(ROWS, COLS, CHANS),
            semaphores(5),
            semaphores(3),
        ],
        flops=2 * 10**9,
    )(gathered1, mean1, mix2, mid, norm_gain, s2, tap_sum2)
    return out


def solution(mesh):
    split = Mesh(mesh.devices.reshape(2, 4, 2, 8, 2), ("mem", "y", "xh", "z", "core"))
    placed = (P(LAT, LON, "mem"), P(), P(), P(None, None, LAT, None, None), P(LAT))
    return jax.shard_map(
        local, mesh=split, in_specs=placed, out_specs=P(LAT, LON, "mem"), check_vma=False
    )
```
